128 devices in a mesh: stn: 32 (over z_hi, y, x), tm: 4 (over z_lo, core).
Axes of the slice: x: 4, y: 4, z: 4 (z_hi: 2, z_lo: 2; z = z_hi * 2 + z_lo), core: 2. Of those that a mesh axis runs over, the one named last changes fastest.
Arguments:
- voltages: bfloat16 [2, 256, 32, 16384], P(None, 'stn', None, 'tm'), may hold values from -6 to 6
Outputs:
- visibilities: float32 [2048, 2, 256, 256], P(('stn', 'tm'))
The draws below stay inside these ranges and needn't reach their ends.
All inputs are finite; a program needn't handle non-finite values.
Results may differ from the reference program's by a relative error of at most 0.0056.
Values may be sent and summed in bfloat16 or wider, within the bound.
No kernel may reach another device: no remote copies, remote signals or barrier semaphores. Data moves between devices by JAX's collectives and lax.ppermute only.
A program may use at most 192 MiB of HBM per device.

```python
import jax
import jax.numpy as jnp
from jax import lax

INPUTS = 256
NFFT = 64
TAPS = 16
COARSE = 32
FINE = 2048
NSPEC = 256
SAMPLES = 16384


def block_levels(rng, shape, pieces, smallest, top_value):
    factor_of = 1.0
    for dim, shards_of in pieces:
        heights = jax.random.uniform(jax.random.fold_in(jax.random.fold_in(rng, 6), dim), (shards_of,), jnp.float32, smallest / len(pieces), top_value / len(pieces))
        factor_of = factor_of * jnp.repeat(jnp.exp(heights), shape[dim] // shards_of).reshape((-1,) + (1,) * (len(shape) - 1 - dim))
    return factor_of


def normal_values(rng, shape, scale, reach, pieces=(), held_as=jnp.bfloat16):
    factor_of = block_levels(rng, shape, pieces, -0.22, 0.18) if pieces else 1.0
    drawn = jax.random.normal(rng, shape, jnp.float32) * scale * factor_of
    return jnp.minimum(jnp.maximum(drawn, -reach), reach).astype(held_as)


def setup_inputs(seed: int = 0) -> dict:
    splits = jax.random.split(jax.random.key(seed), 2)
    return {
        "voltages": normal_values(splits[0], (2, INPUTS, COARSE, SAMPLES), 1.0, 6.0, ((1, 32), (3, 4))),
    }


def make_taps():
    length = TAPS * NFFT
    index = jnp.arange(length, dtype=jnp.float32)
    shape_part = jnp.sinc((index - (length - 1) / 2.0) / NFFT)
    window = 0.5 - 0.5 * jnp.cos(2.0 * jnp.pi * (index + 0.5) / length)
    return (shape_part * window).astype(jnp.float32)

def make_table(flat_taps):
    gain = 1.0 / jnp.sqrt(jnp.sum(flat_taps * flat_taps))
    index = jnp.arange(NFFT, dtype=jnp.int32)
    phase = index[:, None] * index[None, :] % NFFT
    angle = -2.0 * jnp.pi * phase.astype(jnp.float32) / NFFT
    cosine = jnp.cos(angle) * gain
    sine = jnp.sin(angle) * gain
    real_row = jnp.stack([cosine, sine], axis=1)
    imag_row = jnp.stack([-sine, cosine], axis=1)
    return jnp.stack([real_row, imag_row], axis=0).astype(jnp.bfloat16)

def reference(voltages):
    flat_taps = make_taps()
    taps = flat_taps.reshape(TAPS, NFFT)
    table = make_table(flat_taps).astype(jnp.float32)
    history = (TAPS - 1) * NFFT
    scale = 1.0 / NSPEC

    def one_coarse(index):
        samples = lax.dynamic_index_in_dim(voltages, index, 2, keepdims=False)
        padded = jnp.pad(samples, ((0, 0), (0, 0), (history, 0)))
        blocks = padded.reshape(2, INPUTS, NSPEC + TAPS - 1, NFFT)
        filtered = jnp.zeros((2, INPUTS, NSPEC, NFFT), jnp.float32)
        for tap in range(TAPS):
            begin = TAPS - 1 - tap
            filtered = filtered + taps[tap] * blocks[:, :, begin:begin + NSPEC, :].astype(jnp.float32)
        filtered = filtered.astype(jnp.bfloat16).astype(jnp.float32)
        spectra = jnp.einsum('aisn,anbk->biks', filtered, table).astype(jnp.bfloat16)
        real_part = spectra[0].astype(jnp.float32)
        imag_part = spectra[1].astype(jnp.float32)
        joined = jnp.concatenate([real_part, imag_part], axis=-1)
        turned = jnp.concatenate([imag_part, -real_part], axis=-1)
        vis_real = jnp.einsum('iks,jks->kij', joined, joined)
        vis_imag = jnp.einsum('iks,jks->kij', turned, joined)
        return jnp.stack([vis_real, vis_imag], axis=1) * scale
    result = lax.map(one_coarse, jnp.arange(COARSE, dtype=jnp.int32))
    return result.reshape(FINE, 2, INPUTS, INPUTS)
```

```python
import functools

import jax
import jax.numpy as jnp
import ml_dtypes
import numpy as np
from jax import lax
from jax.experimental import pallas as pl
from jax.experimental.pallas import tpu as pltpu
from jax.sharding import PartitionSpec as P

NFFT = 64
TAPS = 16
QUAD = 4
WINDOW = (TAPS + QUAD) * NFFT
HALO = TAPS * NFFT
MIB = 1 << 20


def from_behind(array, axis, by):
    size = lax.axis_size(axis)
    pairs = [(i, i + by) for i in range(size) if 0 <= i + by < size]
    return lax.ppermute(array, axis, pairs)


def make_weights():
    length = TAPS * NFFT
    index = np.arange(length, dtype=np.float64)
    window = 0.5 - 0.5 * np.cos(2.0 * np.pi * (index + 0.5) / length)
    flat = np.sinc((index - (length - 1) / 2.0) / NFFT) * window
    taps = flat.reshape(TAPS, NFFT)
    gain = 1.0 / np.sqrt(np.sum(flat * flat))
    n = np.arange(NFFT)
    angle = -2.0 * np.pi * (n[:, None] * n[None, :] % NFFT) / NFFT
    cosine, sine = np.cos(angle) * gain, np.sin(angle) * gain
    table = np.stack([np.stack([cosine, sine], 1), np.stack([-sine, cosine], 1)], 0)
    table = table.astype(ml_dtypes.bfloat16).astype(np.float64)
    weights = np.zeros((NFFT, 2, QUAD, 2, TAPS + QUAD, NFFT))
    for spec in range(QUAD):
        for tap in range(TAPS):
            part = taps[tap][None, :, None, None] * table
            weights[:, :, spec, :, spec + TAPS - tap, :] = part.transpose(3, 2, 0, 1)
    return weights.reshape(NFFT * 2 * QUAD, 2 * WINDOW).astype(ml_dtypes.bfloat16)


def make_swap(in_dev, coarse):
    size = in_dev * coarse
    swap = np.zeros((size, size))
    for i in range(in_dev):
        for c in range(coarse):
            swap[c * in_dev + i, i * coarse + c] = 1.0
    return swap.astype(ml_dtypes.bfloat16)


NT = (((1,), (1,)), ((), ()))


def channelise_kernel(halo_ref, volt_ref, weight_ref, swap_ref, out_ref, ext_ref, spec_ref):
    step = pl.program_id(0)
    pairs = spec_ref.shape[1] // 16
    rows = ext_ref.shape[1] * ext_ref.shape[2]

    @pl.when(step == 0)
    def _():
        ext_ref[:, :, :, :HALO] = halo_ref[...]
        ext_ref[:, :, :, HALO:] = volt_ref[...]

    @pl.when(step < pairs)
    def _():
        quads = []
        for half in range(2):
            begin = pl.multiple_of((2 * step + half) * QUAD * NFFT, 128)
            total = None
            for part in range(2):
                block = ext_ref[part, :, :, pl.ds(begin, WINDOW)].reshape(rows, WINDOW)
                weight = weight_ref[:, part * WINDOW : (part + 1) * WINDOW]
                term = lax.dot_general(weight, block, NT, preferred_element_type=jnp.float32)
                total = term if total is None else total + term
            quads.append(total.reshape(NFFT, 2 * QUAD, rows))
        both = jnp.concatenate(quads, axis=1).astype(jnp.bfloat16)
        spec_ref[:, pl.ds(pl.multiple_of(step * 16, 16), 16), :] = both

    @pl.when(step >= pairs)
    def _():
        per = out_ref.shape[2]
        base = (step - pairs) * 2 * per
        for pair in range(per):
            both = []
            for one in range(2):
                block = spec_ref[base + 2 * pair + one]
                turned = lax.dot_general(
                    swap_ref[...], block, NT, preferred_element_type=jnp.float32
                )
                both.append(turned.reshape(out_ref.shape[0], 8, 128))
            out_ref[:, 0, pair] = jnp.concatenate(both, axis=1).astype(jnp.bfloat16)


def channelise(halo, voltages):
    _, in_dev, coarse, samples = voltages.shape
    pairs = samples // NFFT // (2 * QUAD)
    weights = jnp.asarray(make_weights())
    swap = jnp.asarray(make_swap(in_dev, coarse))
    whole = lambda shape: pl.BlockSpec(shape, lambda s: (0,) * len(shape))
    return pl.pallas_call(
        channelise_kernel,
        grid=(pairs + 8,),
        in_specs=[whole(halo.shape), whole(voltages.shape), whole(weights.shape), whole(swap.shape)],
        out_specs=pl.BlockSpec(
            (coarse, 1, 4, 16, 128),
            lambda s: (0, jnp.maximum(s - pairs, 0) // 2, jnp.maximum(s - pairs, 0) % 2, 0, 0),
        ),
        out_shape=jax.ShapeDtypeStruct((coarse, 4, 8, 16, 128), jnp.bfloat16),
        scratch_shapes=[
            pltpu.VMEM((2, in_dev, coarse, HALO + samples), jnp.bfloat16),
            pltpu.VMEM((NFFT, pairs * 16, in_dev * coarse), jnp.bfloat16),
        ],
        compiler_params=pltpu.CompilerParams(vmem_limit_bytes=48 * MIB),
        cost_estimate=pl.CostEstimate(
            flops=2 * 512 * 2560 * 256 * 16, bytes_accessed=12 * MIB, transcendentals=0
        ),
        name="channelise",
    )(halo, voltages, weights, swap)


def correlate_kernel(scale, spec_ref, out_ref):
    sources = spec_ref.shape[0]
    stations = sources // 4
    inputs = stations * 8
    block = spec_ref[:, 0].astype(jnp.float32).reshape(stations, 4, 2, 8, 128)
    lane = lax.broadcasted_iota(jnp.int32, (inputs, 128), 1)
    is_real = lane % (2 * QUAD) < QUAD
    for one in range(2):
        joined, turned = [], []
        for part in range(4):
            plain = block[:, part, one].reshape(inputs, 128)
            ahead = pltpu.roll(plain, 128 - QUAD, 1)
            behind = pltpu.roll(plain, QUAD, 1)
            joined.append(plain.astype(jnp.bfloat16))
            turned.append(jnp.where(is_real, ahead, -behind).astype(jnp.bfloat16))
        joined = jnp.concatenate(joined, axis=1)
        turned = jnp.concatenate(turned, axis=1)
        out_ref[one, 0] = (
            lax.dot_general(joined, joined, NT, preferred_element_type=jnp.float32) * scale
        )
        out_ref[one, 1] = (
            lax.dot_general(turned, joined, NT, preferred_element_type=jnp.float32) * scale
        )


def correlate(spectra, scale):
    sources = spectra.shape[0]
    inputs = sources // 4 * 8
    return pl.pallas_call(
        functools.partial(correlate_kernel, scale),
        grid=(8,),
        in_specs=[pl.BlockSpec((sources, 1, 16, 128), lambda s: (0, s, 0, 0))],
        out_specs=pl.BlockSpec((2, 2, inputs, inputs), lambda s: (s, 0, 0, 0)),
        out_shape=jax.ShapeDtypeStruct((16, 2, inputs, inputs), jnp.float32),
        compiler_params=pltpu.CompilerParams(vmem_limit_bytes=32 * MIB),
        cost_estimate=pl.CostEstimate(
            flops=2 * 16 * 2 * 256 * 256 * 512, bytes_accessed=12 * MIB, transcendentals=0
        ),
        name="correlate",
    )(spectra)


def body(voltages):
    samples = voltages.shape[3]
    scale = NFFT / (lax.axis_size("tm") * samples)
    halo = from_behind(voltages[:, :, :, samples - HALO :], "tm", 1)
    spectra = channelise(halo, voltages)
    spectra = spectra.reshape(128, 8, 16, 128)
    moved = lax.all_to_all(spectra, ("stn", "tm"), split_axis=0, concat_axis=0, tiled=True)
    return correlate(moved, scale)


def solution(mesh):
    placed = (P(None, "stn", None, "tm"),)
    return jax.shard_map(
        body,
        mesh=mesh,
        in_specs=placed,
        out_specs=P(("stn", "tm"), None, None, None),
        check_vma=False,
    )
```

```python
import functools

import jax
import jax.numpy as jnp
import ml_dtypes
import numpy as np
from jax import lax
from jax.experimental import pallas as pl
from jax.experimental.pallas import tpu as pltpu
from jax.sharding import PartitionSpec as P

NFFT = 64
TAPS = 16
QUAD = 4
OCTET = 2 * QUAD * NFFT
WINDOW = (TAPS + QUAD) * NFFT
HALO = TAPS * NFFT
MIB = 1 << 20
NT = (((1,), (1,)), ((), ()))


def from_behind(array, axis, by):
    size = lax.axis_size(axis)
    pairs = [(i, i + by) for i in range(size) if 0 <= i + by < size]
    return lax.ppermute(array, axis, pairs)


def make_weights():
    length = TAPS * NFFT
    index = np.arange(length, dtype=np.float64)
    window = 0.5 - 0.5 * np.cos(2.0 * np.pi * (index + 0.5) / length)
    flat = np.sinc((index - (length - 1) / 2.0) / NFFT) * window
    taps = flat.reshape(TAPS, NFFT)
    gain = 1.0 / np.sqrt(np.sum(flat * flat))
    n = np.arange(NFFT)
    angle = -2.0 * np.pi * (n[:, None] * n[None, :] % NFFT) / NFFT
    cosine, sine = np.cos(angle) * gain, np.sin(angle) * gain
    table = np.stack([np.stack([cosine, sine], 1), np.stack([-sine, cosine], 1)], 0)
    table = table.astype(ml_dtypes.bfloat16).astype(np.float64)
    rows = table[:, :, :, : NFFT // 2].copy()
    rows[0, :, 1, 0] = table[0, :, 0, NFFT // 2]
    rows[1, :, 0, 0] = table[1, :, 1, NFFT // 2]
    weights = np.zeros((NFFT // 2, 2, QUAD, 2, TAPS + QUAD, NFFT))
    for spec in range(QUAD):
        for tap in range(TAPS):
            part = taps[tap][None, :, None, None] * rows
            weights[:, :, spec, :, spec + TAPS - tap, :] = part.transpose(3, 2, 0, 1)
    return weights.reshape(NFFT * QUAD, 2 * WINDOW).astype(ml_dtypes.bfloat16)


def make_swap(in_dev, coarse):
    size = in_dev * coarse
    swap = np.zeros((size, size))
    for i in range(in_dev):
        for c in range(coarse):
            swap[c * in_dev + i, i * coarse + c] = 1.0
    return swap.astype(ml_dtypes.bfloat16)


def channels_of(blocks, weight_ref, store):
    rows = blocks[0].shape[1] * blocks[0].shape[2]
    joined = [
        jnp.concatenate([block[part].reshape(rows, OCTET) for block in blocks], axis=1)
        for part in range(2)
    ]
    plus, minus = [], []
    upper = lax.broadcasted_iota(jnp.int32, (8, rows), 0) < QUAD
    for half in range(2):
        begin = half * QUAD * NFFT
        terms = [
            lax.dot_general(
                weight_ref[:, part * WINDOW : (part + 1) * WINDOW],
                joined[part][:, begin : begin + WINDOW],
                NT,
                preferred_element_type=jnp.float32,
            ).reshape(NFFT // 2, 8, rows)
            for part in range(2)
        ]
        low = jnp.where(upper, terms[0][0], terms[1][0])
        high = jnp.where(upper, terms[1][0], terms[0][0])
        plus.append([low] + [terms[0][k] + terms[1][k] for k in range(1, NFFT // 2)])
        minus.append(
            [pltpu.roll(high, QUAD, 0)]
            + [
                jnp.where(upper, terms[0][k] - terms[1][k], terms[1][k] - terms[0][k])
                for k in range(1, NFFT // 2)
            ]
        )
    for k in range(NFFT // 2):
        store(k, jnp.concatenate([plus[0][k], plus[1][k]], axis=0).astype(jnp.bfloat16))
        mirror = NFFT - k if k else NFFT // 2
        store(mirror, jnp.concatenate([minus[0][k], minus[1][k]], axis=0).astype(jnp.bfloat16))


def copies_in(pairs, sems):
    copies = [pltpu.make_async_copy(src, dst, sems.at[i]) for i, (src, dst) in enumerate(pairs)]
    for copy in copies:
        copy.start()
    return copies


def turn_pair(swap_ref, block, out_shape):
    turned = lax.dot_general(swap_ref[...], block, NT, preferred_element_type=jnp.float32)
    return [turned[:, one * 128 : (one + 1) * 128].reshape(out_shape) for one in range(2)]


def late_kernel(volt_ref, weight_hbm, swap_hbm, out_ref, ext_ref, weight_ref, swap_ref, spec_ref, sems):
    octets = ext_ref.shape[3] // OCTET
    pieces = [pl.ds(o * OCTET, OCTET) for o in range(octets)]
    copies = copies_in(
        [(weight_hbm, weight_ref)]
        + [(volt_ref.at[:, :, :, piece], ext_ref.at[:, :, :, piece]) for piece in pieces]
        + [(swap_hbm, swap_ref)],
        sems,
    )
    rows = spec_ref.shape[2]
    for k in range(NFFT):
        gap = 32 * (k % 4)
        spec_ref[k, gap : gap + 32] = jnp.zeros((32, rows), jnp.bfloat16)
    copies[0].wait()
    for o in range(2):
        copies[1 + o].wait()
    for o in range(octets - 2):
        copies[3 + o].wait()

        def store(k, value):
            row = 16 * (o + (2 if o >= 2 * (k % 4) else 0))
            spec_ref[k, row : row + 16] = value

        channels_of(
            [ext_ref[:, :, :, (o + j) * OCTET : (o + j + 1) * OCTET] for j in range(3)],
            weight_ref,
            store,
        )
    copies[-1].wait()
    coarse, pairs = out_ref.shape[:2]

    def turn(pair, carry):
        block = spec_ref[pl.ds(2 * pair, 2)].reshape(256, rows)
        both = turn_pair(swap_ref, block, (coarse, 8, 128))
        out_ref[:, pair] = jnp.concatenate(both, axis=1).astype(jnp.bfloat16)
        return carry

    lax.fori_loop(0, pairs, turn, 0, unroll=8)


def early_kernel(halo_ref, volt_ref, weight_ref, swap_ref, late_ref, out_ref, spec_ref):
    pieces = [ref[:, :, :, o * OCTET : (o + 1) * OCTET] for ref in (halo_ref, volt_ref) for o in range(2)]
    for octet in range(2):

        def store(k, value):
            row = 32 * (k % 4) + 16 * octet
            spec_ref[k // 4, row : row + 16] = value

        channels_of(pieces[octet : octet + 3], weight_ref, store)
    coarse = out_ref.shape[0]
    rows = spec_ref.shape[2]
    lane = lax.broadcasted_iota(jnp.int32, (16, 128), 1)
    second = lax.broadcasted_iota(jnp.int32, (16, 128), 0) // 8
    masks = [
        jnp.where(lane // 32 == 2 * p + second, 1.0, 0.0).astype(jnp.bfloat16) for p in range(2)
    ]

    def turn(two, carry):
        block = spec_ref[pl.ds(2 * two, 2)].reshape(256, rows)
        for one, part in enumerate(turn_pair(swap_ref, block, (coarse, 8, 128))):
            both = jnp.concatenate([part, part], axis=1).astype(jnp.bfloat16)
            for p in range(2):
                pair = (2 * two + one) * 2 + p
                out_ref[:, pair] = late_ref[:, pair] + both * masks[p]
        return carry

    lax.fori_loop(0, spec_ref.shape[0] // 2, turn, 0, unroll=4)


def channelise_late(voltages):
    _, in_dev, coarse, samples = voltages.shape
    octets = samples // OCTET
    weights = jnp.asarray(make_weights())
    swap = jnp.asarray(make_swap(in_dev, coarse))
    return pl.pallas_call(
        late_kernel,
        in_specs=[pl.BlockSpec(memory_space=pltpu.HBM)] * 3,
        out_specs=pl.BlockSpec(memory_space=pltpu.VMEM),
        out_shape=jax.ShapeDtypeStruct((coarse, 32, 16, 128), jnp.bfloat16),
        scratch_shapes=[
            pltpu.VMEM(voltages.shape, jnp.bfloat16),
            pltpu.VMEM(weights.shape, jnp.bfloat16),
            pltpu.VMEM(swap.shape, jnp.bfloat16),
            pltpu.VMEM((NFFT, 128, in_dev * coarse), jnp.bfloat16),
            pltpu.SemaphoreType.DMA((octets + 2,)),
        ],
        compiler_params=pltpu.CompilerParams(vmem_limit_bytes=32 * MIB),
        cost_estimate=pl.CostEstimate(
            flops=2 * 256 * 2560 * 256 * 12, bytes_accessed=10 * MIB, transcendentals=0
        ),
        name="channelise_late",
    )(voltages, weights, swap)


def channelise_early(halo, voltages, late):
    _, in_dev, coarse, samples = voltages.shape
    weights = jnp.asarray(make_weights())
    swap = jnp.asarray(make_swap(in_dev, coarse))
    whole = pl.BlockSpec(memory_space=pltpu.VMEM)
    return pl.pallas_call(
        early_kernel,
        grid=(1,),
        in_specs=[
            whole,
            pl.BlockSpec((2, in_dev, coarse, 2 * OCTET), lambda s: (0, 0, 0, 0)),
            whole,
            whole,
            whole,
        ],
        out_specs=whole,
        out_shape=jax.ShapeDtypeStruct(late.shape, jnp.bfloat16),
        scratch_shapes=[pltpu.VMEM((NFFT // 4, 128, in_dev * coarse), jnp.bfloat16)],
        compiler_params=pltpu.CompilerParams(vmem_limit_bytes=32 * MIB),
        cost_estimate=pl.CostEstimate(
            flops=2 * 256 * 2560 * 256 * 4, bytes_accessed=12 * MIB, transcendentals=0
        ),
        name="channelise_early",
    )(halo, voltages, weights, swap, late)


def correlate_kernel(scale, spec_ref, out_hbm, stage_ref, sems):
    sources, pairs = spec_ref.shape[:2]
    stations = sources // 4
    inputs = stations * 8
    lane = lax.broadcasted_iota(jnp.int32, (inputs, 128), 1)
    is_real = lane % (2 * QUAD) < QUAD

    def copy(pair):
        at = pl.ds(2 * pair, 2)
        return pltpu.make_async_copy(stage_ref.at[at], out_hbm.at[at], sems.at[pair])

    def one_pair(pair, carry):
        block = spec_ref[:, pair].astype(jnp.float32).reshape(stations, 4, 2, 8, 128)
        for one in range(2):
            joined, turned = [], []
            for part in range(4):
                plain = block[:, part, one].reshape(inputs, 128)
                ahead = pltpu.roll(plain, 128 - QUAD, 1)
                behind = pltpu.roll(plain, QUAD, 1)
                joined.append(plain.astype(jnp.bfloat16))
                turned.append(jnp.where(is_real, ahead, -behind).astype(jnp.bfloat16))
            joined = jnp.concatenate(joined, axis=1)
            turned = jnp.concatenate(turned, axis=1)
            for which, left in enumerate((joined, turned)):
                power = lax.dot_general(left, joined, NT, preferred_element_type=jnp.float32)
                stage_ref[2 * pair + one, which] = power * scale
        copy(pair).start()
        return carry

    lax.fori_loop(0, pairs, one_pair, 0, unroll=2)
    for pair in range(pairs):
        copy(pair).wait()


def correlate(spectra, scale):
    sources, pairs = spectra.shape[:2]
    inputs = sources // 4 * 8
    shape = (2 * pairs, 2, inputs, inputs)
    return pl.pallas_call(
        functools.partial(correlate_kernel, scale),
        in_specs=[pl.BlockSpec(memory_space=pltpu.VMEM)],
        out_specs=pl.BlockSpec(memory_space=pltpu.HBM),
        out_shape=jax.ShapeDtypeStruct(shape, jnp.float32),
        scratch_shapes=[
            pltpu.VMEM(shape, jnp.float32),
            pltpu.SemaphoreType.DMA((pairs,)),
        ],
        compiler_params=pltpu.CompilerParams(vmem_limit_bytes=32 * MIB),
        cost_estimate=pl.CostEstimate(
            flops=2 * 16 * 2 * 256 * 256 * 512, bytes_accessed=12 * MIB, transcendentals=0
        ),
        name="correlate",
    )(spectra)


def body(voltages):
    samples = voltages.shape[3]
    scale = NFFT / (lax.axis_size("tm") * samples)
    halo = from_behind(voltages[:, :, :, samples - HALO :], "tm", 1)
    late = channelise_late(voltages)
    spectra = channelise_early(halo, voltages, late)
    spectra = spectra.reshape(128, 8, 16, 128)
    moved = lax.all_to_all(spectra, ("stn", "tm"), split_axis=0, concat_axis=0, tiled=True)
    return correlate(moved, scale)


def solution(mesh):
    placed = (P(None, "stn", None, "tm"),)
    return jax.shard_map(
        body,
        mesh=mesh,
        in_specs=placed,
        out_specs=P(("stn", "tm"), None, None, None),
        check_vma=False,
    )
```

```python
import functools

import jax
import jax.numpy as jnp
import ml_dtypes
import numpy as np
from jax import lax
from jax.experimental import pallas as pl
from jax.experimental.pallas import tpu as pltpu
from jax.sharding import PartitionSpec as P

NFFT = 64
TAPS = 16
QUAD = 4
OCTET = 2 * QUAD * NFFT
WINDOW = (TAPS + QUAD) * NFFT
HALO = TAPS * NFFT
MIB = 1 << 20
NT = (((1,), (1,)), ((), ()))
STATION = ("z_hi", "y", "x")
TIME = ("z_lo", "core")


def from_behind(array, axis, by):
    size = lax.axis_size(axis)
    return lax.ppermute(array, axis, [(i, (i + by) % size) for i in range(size)])


def make_weights():
    length = TAPS * NFFT
    index = np.arange(length, dtype=np.float64)
    window = 0.5 - 0.5 * np.cos(2.0 * np.pi * (index + 0.5) / length)
    flat = np.sinc((index - (length - 1) / 2.0) / NFFT) * window
    taps = flat.reshape(TAPS, NFFT)
    gain = 1.0 / np.sqrt(np.sum(flat * flat))
    n = np.arange(NFFT)
    angle = -2.0 * np.pi * (n[:, None] * n[None, :] % NFFT) / NFFT
    cosine, sine = np.cos(angle) * gain, np.sin(angle) * gain
    table = np.stack([np.stack([cosine, sine], 1), np.stack([-sine, cosine], 1)], 0)
    table = table.astype(ml_dtypes.bfloat16).astype(np.float64)
    rows = table[:, :, :, : NFFT // 2].copy()
    rows[0, :, 1, 0] = table[0, :, 0, NFFT // 2]
    rows[1, :, 0, 0] = table[1, :, 1, NFFT // 2]
    weights = np.zeros((NFFT // 2, 2, QUAD, 2, TAPS + QUAD, NFFT))
    for spec in range(QUAD):
        for tap in range(TAPS):
            part = taps[tap][None, :, None, None] * rows
            weights[:, :, spec, :, spec + TAPS - tap, :] = part.transpose(3, 2, 0, 1)
    return weights.reshape(NFFT * QUAD, 2 * WINDOW).astype(ml_dtypes.bfloat16)


def make_swap(in_dev, coarse):
    size = in_dev * coarse
    swap = np.zeros((size, size))
    for i in range(in_dev):
        for c in range(coarse):
            swap[c * in_dev + i, i * coarse + c] = 1.0
    return swap.astype(ml_dtypes.bfloat16)


def quad_channels(samples, begin, width, const_ref, first):
    rows = samples[0].shape[0] * samples[0].shape[1]
    terms = [
        lax.dot_general(
            const_ref[:, part * WINDOW + first : part * WINDOW + first + width],
            samples[part][:, :, begin : begin + width].reshape(rows, width),
            NT,
            preferred_element_type=jnp.float32,
        ).reshape(NFFT // 2, 8, rows)
        for part in range(2)
    ]
    upper = lax.broadcasted_iota(jnp.int32, (8, rows), 0) < QUAD
    channels = [None] * NFFT
    channels[0] = jnp.where(upper, terms[0][0], terms[1][0])
    channels[NFFT // 2] = pltpu.roll(jnp.where(upper, terms[1][0], terms[0][0]), QUAD, 0)
    for k in range(1, NFFT // 2):
        channels[k] = terms[0][k] + terms[1][k]
        difference = terms[0][k] - terms[1][k]
        channels[NFFT - k] = jnp.where(upper, difference, -difference)
    return channels


def turn_pair(const_ref, block, out_shape):
    swap = const_ref[:, 2 * WINDOW :]
    turned = lax.dot_general(swap, block, NT, preferred_element_type=jnp.float32)
    return [turned[:, one * 128 : (one + 1) * 128].reshape(out_shape) for one in range(2)]


def late_kernel(volt_ref, const_ref, out_ref, own_ref, spec_ref):
    octets = volt_ref.shape[3] // OCTET
    own = [volt_ref.at[part] for part in range(2)]
    rows = spec_ref.shape[2]
    step = QUAD * NFFT
    for k in range(NFFT):
        gap = 32 * (k % 4)
        spec_ref[k, gap : gap + 32] = jnp.zeros((32, rows), jnp.bfloat16)
    for octet in range(2, octets):
        quads = [
            quad_channels(own, (2 * octet + half) * step - HALO, WINDOW, const_ref, 0)
            for half in range(2)
        ]
        for k in range(NFFT):
            row = 16 * (octet - (0 if octet - 2 >= 2 * (k % 4) else 2))
            both = jnp.concatenate([quads[0][k], quads[1][k]], axis=0)
            spec_ref[k, row : row + 16] = both.astype(jnp.bfloat16)
    coarse = rows // 8

    for z_lo in range(2):

        def turn(pair, carry):
            block = spec_ref[pl.ds(32 * z_lo + 2 * pair, 2)].reshape(256, rows)
            both = turn_pair(const_ref, block, (coarse, 8, 128))
            both = jnp.concatenate(both, axis=1).astype(jnp.bfloat16)
            out_ref[:, z_lo, :, pair] = both.reshape(2, coarse // 2, 16, 128)
            return carry

        lax.fori_loop(0, NFFT // 4, turn, 0, unroll=8)
    for quad in range(4):
        width = (quad + 1) * step
        channels = quad_channels(own, 0, width, const_ref, WINDOW - width)
        for k in range(NFFT):
            own_ref[k, 8 * quad : 8 * quad + 8] = channels[k]


def early_kernel(real_ref, imag_ref, const_ref, late_ref, own_ref, out_ref, spec_ref):
    step = QUAD * NFFT
    keep = jnp.where(lax.axis_index(TIME) == 0, 0.0, 1.0)
    for octet in range(2):
        quads = []
        for half in range(2):
            begin = (2 * octet + half) * step
            quads.append(quad_channels([real_ref, imag_ref], begin, HALO - begin, const_ref, 0))
        for k in range(NFFT):
            row = 32 * (k % 4) + 16 * octet
            both = jnp.concatenate([quads[0][k], quads[1][k]], axis=0)
            both = both * keep + own_ref[k, 16 * octet : 16 * octet + 16]
            spec_ref[k // 4, row : row + 16] = both.astype(jnp.bfloat16)
    rows = spec_ref.shape[2]
    coarse = rows // 8
    lane = lax.broadcasted_iota(jnp.int32, (16, 128), 1)
    second = lax.broadcasted_iota(jnp.int32, (16, 128), 0) // 8
    masks = [
        jnp.where(lane // 32 == 2 * p + second, 1.0, 0.0).astype(jnp.bfloat16) for p in range(2)
    ]

    for two in range(spec_ref.shape[0] // 2):
        block = spec_ref[2 * two : 2 * two + 2].reshape(256, rows)
        for one, part in enumerate(turn_pair(const_ref, block, (coarse, 8, 128))):
            both = jnp.concatenate([part, part], axis=1).astype(jnp.bfloat16)
            for p in range(2):
                pair = (2 * two + one) * 2 + p
                placed = (both * masks[p]).reshape(2, coarse // 2, 16, 128)
                at = (slice(None), pair // 16, slice(None), pair % 16)
                out_ref[at] = late_ref[at] + placed


VMEM = pl.BlockSpec(memory_space=pltpu.VMEM)


def channelise_late(voltages, const):
    _, in_dev, coarse, samples = voltages.shape
    rows = in_dev * coarse
    return pl.pallas_call(
        late_kernel,
        in_specs=[VMEM, VMEM],
        out_specs=[VMEM, VMEM],
        out_shape=[
            jax.ShapeDtypeStruct((2, 2, coarse // 2, 16, 16, 128), jnp.bfloat16),
            jax.ShapeDtypeStruct((NFFT, 32, rows), jnp.float32),
        ],
        scratch_shapes=[pltpu.VMEM((NFFT, 128, rows), jnp.bfloat16)],
        compiler_params=pltpu.CompilerParams(vmem_limit_bytes=24 * MIB),
        cost_estimate=pl.CostEstimate(
            flops=2 * 256 * 2560 * 256 * 12, bytes_accessed=10 * MIB, transcendentals=0
        ),
        name="channelise_late",
    )(voltages, const)


def channelise_early(real, imag, const, late, own):
    rows = own.shape[2]
    return pl.pallas_call(
        early_kernel,
        in_specs=[VMEM] * 5,
        out_specs=VMEM,
        out_shape=jax.ShapeDtypeStruct(late.shape, jnp.bfloat16),
        scratch_shapes=[pltpu.VMEM((NFFT // 4, 128, rows), jnp.bfloat16)],
        compiler_params=pltpu.CompilerParams(vmem_limit_bytes=24 * MIB),
        cost_estimate=pl.CostEstimate(
            flops=2 * 256 * 1280 * 256 * 4, bytes_accessed=12 * MIB, transcendentals=0
        ),
        name="channelise_early",
    )(real, imag, const, late, own)


def correlate_kernel(scale, spec_ref, out_hbm, stage_ref, sems):
    sources, pairs = spec_ref.shape[:2]
    inputs = sources // 4 * 8
    lane = lax.broadcasted_iota(jnp.int32, (inputs, 128), 1)
    is_real = lane % (2 * QUAD) < QUAD

    def copy(channel):
        return pltpu.make_async_copy(stage_ref.at[channel], out_hbm.at[channel], sems.at[channel])

    def one_pair(pair, carry):
        block = spec_ref[:, pair].astype(jnp.float32).reshape(2, 2, sources // 8, 2, 2, 8, 128)
        for one in range(2):
            joined, turned = [], []
            for z_lo in range(2):
                for core in range(2):
                    plain = block[:, z_lo, :, core, one].reshape(inputs, 128)
                    ahead = pltpu.roll(plain, 128 - QUAD, 1)
                    behind = pltpu.roll(plain, QUAD, 1)
                    joined.append(plain.astype(jnp.bfloat16))
                    turned.append(jnp.where(is_real, ahead, -behind).astype(jnp.bfloat16))
            joined = jnp.concatenate(joined, axis=1)
            turned = jnp.concatenate(turned, axis=1)
            channel = 2 * pair + one
            for which, left in enumerate((joined, turned)):
                power = lax.dot_general(left, joined, NT, preferred_element_type=jnp.float32)
                stage_ref[channel, which] = power * scale
            copy(channel).start()
        return carry

    lax.fori_loop(0, pairs, one_pair, 0, unroll=4)
    for channel in range(2 * pairs):
        copy(channel).wait()


def correlate(spectra, scale):
    sources, pairs = spectra.shape[:2]
    inputs = sources // 4 * 8
    shape = (2 * pairs, 2, inputs, inputs)
    return pl.pallas_call(
        functools.partial(correlate_kernel, scale),
        in_specs=[pl.BlockSpec(memory_space=pltpu.VMEM)],
        out_specs=pl.BlockSpec(memory_space=pltpu.HBM),
        out_shape=jax.ShapeDtypeStruct(shape, jnp.float32),
        scratch_shapes=[
            pltpu.VMEM(shape, jnp.float32),
            pltpu.SemaphoreType.DMA((2 * pairs,)),
        ],
        compiler_params=pltpu.CompilerParams(vmem_limit_bytes=32 * MIB),
        cost_estimate=pl.CostEstimate(
            flops=2 * 16 * 2 * 256 * 256 * 512, bytes_accessed=12 * MIB, transcendentals=0
        ),
        name="correlate",
    )(spectra)


def body(voltages):
    samples = voltages.shape[3]
    scale = NFFT / (lax.axis_size(TIME) * samples)
    const = jnp.asarray(
        np.concatenate([make_weights(), make_swap(*voltages.shape[1:3])], axis=1)
    )
    begin = samples - HALO
    real, imag = (from_behind(voltages[part, :, :, begin:], TIME, 1) for part in range(2))
    late, own = channelise_late(voltages, const)
    spectra = channelise_early(real, imag, const, late, own)
    spectra = spectra.reshape(128, 8, 16, 128)
    order = ("z_hi", "z_lo", "y", "x", "core")
    moved = lax.all_to_all(spectra, order, split_axis=0, concat_axis=0, tiled=True)
    return correlate(moved, scale)


def solution(mesh):
    mesh = jax.sharding.Mesh(
        mesh.devices.reshape(2, 4, 4, 2, 2), ("z_hi", "y", "x", "z_lo", "core")
    )
    return jax.shard_map(
        body,
        mesh=mesh,
        in_specs=(P(None, STATION, None, TIME),),
        out_specs=P(STATION + TIME, None, None, None),
        check_vma=False,
    )
```

```python
import functools

import jax
import jax.numpy as jnp
import ml_dtypes
import numpy as np
from jax import lax
from jax.experimental import pallas as pl
from jax.experimental.pallas import tpu as pltpu
from jax.sharding import PartitionSpec as P

NFFT = 64
TAPS = 16
QUAD = 4
OCTET = 2 * QUAD * NFFT
WINDOW = (TAPS + QUAD) * NFFT
HALO = TAPS * NFFT
MIB = 1 << 20
NT = (((1,), (1,)), ((), ()))
STATION = ("z_hi", "y", "x")
TIME = ("z_lo", "core")
PLANES_DOWN = [
    ((z_hi * 16 + chip) * 2 + z_lo) * 2 + core
    for z_hi in (1, 0)
    for z_lo in (1, 0)
    for chip in range(16)
    for core in range(2)
]


def from_behind(array, axis, by):
    size = lax.axis_size(axis)
    return lax.ppermute(array, axis, [(i, (i + by) % size) for i in range(size)])


def make_weights():
    length = TAPS * NFFT
    index = np.arange(length, dtype=np.float64)
    window = 0.5 - 0.5 * np.cos(2.0 * np.pi * (index + 0.5) / length)
    flat = np.sinc((index - (length - 1) / 2.0) / NFFT) * window
    taps = flat.reshape(TAPS, NFFT)
    gain = 1.0 / np.sqrt(np.sum(flat * flat))
    n = np.arange(NFFT)
    angle = -2.0 * np.pi * (n[:, None] * n[None, :] % NFFT) / NFFT
    cosine, sine = np.cos(angle) * gain, np.sin(angle) * gain
    table = np.stack([np.stack([cosine, sine], 1), np.stack([-sine, cosine], 1)], 0)
    table = table.astype(ml_dtypes.bfloat16).astype(np.float64)
    rows = table[:, :, :, : NFFT // 2].copy()
    rows[0, :, 1, 0] = table[0, :, 0, NFFT // 2]
    rows[1, :, 0, 0] = table[1, :, 1, NFFT // 2]
    weights = np.zeros((NFFT // 2, 2, QUAD, 2, TAPS + QUAD, NFFT))
    for spec in range(QUAD):
        for tap in range(TAPS):
            part = taps[tap][None, :, None, None] * rows
            weights[:, :, spec, :, spec + TAPS - tap, :] = part.transpose(3, 2, 0, 1)
    return weights.reshape(NFFT * QUAD, 2 * WINDOW).astype(ml_dtypes.bfloat16)


def make_swap(in_dev, coarse):
    size = in_dev * coarse
    swap = np.zeros((size, size))
    for i in range(in_dev):
        for c in range(coarse):
            swap[(c + coarse // 2) % coarse * in_dev + i, i * coarse + c] = 1.0
    return swap.astype(ml_dtypes.bfloat16)


def quad_channels(samples, begin, width, const_ref, first):
    rows = samples[0].shape[0] * samples[0].shape[1]
    terms = [
        lax.dot_general(
            const_ref[:, part * WINDOW + first : part * WINDOW + first + width],
            samples[part][:, :, begin : begin + width].reshape(rows, width),
            NT,
            preferred_element_type=jnp.float32,
        ).reshape(NFFT // 2, 8, rows)
        for part in range(2)
    ]
    upper = lax.broadcasted_iota(jnp.int32, (8, rows), 0) < QUAD
    channels = [None] * NFFT
    channels[0] = jnp.where(upper, terms[0][0], terms[1][0])
    channels[NFFT // 2] = pltpu.roll(jnp.where(upper, terms[1][0], terms[0][0]), QUAD, 0)
    for k in range(1, NFFT // 2):
        channels[k] = terms[0][k] + terms[1][k]
        difference = terms[0][k] - terms[1][k]
        channels[NFFT - k] = jnp.where(upper, difference, -difference)
    return channels


def turn_pair(const_ref, block, out_shape):
    swap = const_ref[:, 2 * WINDOW :]
    turned = lax.dot_general(swap, block, NT, preferred_element_type=jnp.float32)
    return [turned[:, one * 128 : (one + 1) * 128].reshape(out_shape) for one in range(2)]


def late_kernel(volt_ref, const_ref, out_ref, own_ref, spec_ref):
    octets = volt_ref.shape[3] // OCTET
    own = [volt_ref.at[part] for part in range(2)]
    rows = spec_ref.shape[2]
    step = QUAD * NFFT
    for k in range(NFFT):
        gap = 32 * (k % 4)
        spec_ref[k, gap : gap + 32] = jnp.zeros((32, rows), jnp.bfloat16)
    for octet in range(2, octets):
        quads = [
            quad_channels(own, (2 * octet + half) * step - HALO, WINDOW, const_ref, 0)
            for half in range(2)
        ]
        for k in range(NFFT):
            row = 16 * (octet - (0 if octet - 2 >= 2 * (k % 4) else 2))
            both = jnp.concatenate([quads[0][k], quads[1][k]], axis=0)
            spec_ref[k, row : row + 16] = both.astype(jnp.bfloat16)
    coarse = rows // 8

    for z_lo in range(2):

        def turn(pair, carry):
            block = spec_ref[pl.ds(32 * z_lo + 2 * pair, 2)].reshape(256, rows)
            both = turn_pair(const_ref, block, (coarse, 8, 128))
            both = jnp.concatenate(both, axis=1).astype(jnp.bfloat16)
            out_ref[:, 1 - z_lo, :, pair] = both.reshape(2, coarse // 2, 16, 128)
            return carry

        lax.fori_loop(0, NFFT // 4, turn, 0, unroll=8)
    for quad in range(4):
        width = (quad + 1) * step
        channels = quad_channels(own, 0, width, const_ref, WINDOW - width)
        for k in range(NFFT):
            own_ref[k, 8 * quad : 8 * quad + 8] = channels[k]


def keep_halo():
    return jnp.where(lax.axis_index(TIME) == 0, 0.0, 1.0)


def near_kernel(near_ref, const_ref, own_ref, part_ref, whole_ref):
    step = QUAD * NFFT
    near = [near_ref.at[part] for part in range(2)]
    keep = keep_halo()
    first = [
        quad_channels(near, 0, 2 * step, const_ref, (2 - quad) * step) for quad in range(2)
    ]
    second = [
        quad_channels(near, quad * step, (2 - quad) * step, const_ref, 0) for quad in range(2)
    ]
    for k in range(NFFT):
        both = jnp.concatenate([first[0][k], first[1][k]], axis=0)
        part_ref[k] = both * keep + own_ref[k, :16]
        both = jnp.concatenate([second[0][k], second[1][k]], axis=0)
        whole_ref[k] = (both * keep + own_ref[k, 16:]).astype(jnp.bfloat16)


def far_kernel(far_ref, const_ref, late_ref, part_ref, whole_ref, out_ref):
    step = QUAD * NFFT
    far = [far_ref.at[part] for part in range(2)]
    keep = keep_halo()
    quads = [
        quad_channels(far, quad * step, (2 - quad) * step, const_ref, 0) for quad in range(2)
    ]
    rows = part_ref.shape[2]
    coarse = rows // 8
    lane = lax.broadcasted_iota(jnp.int32, (16, 128), 1)
    second = lax.broadcasted_iota(jnp.int32, (16, 128), 0) // 8
    masks = [
        jnp.where(lane // 32 == 2 * p + second, 1.0, 0.0).astype(jnp.bfloat16) for p in range(2)
    ]
    for eight in range(NFFT // 8):
        pieces = []
        for k in range(8 * eight, 8 * eight + 8):
            both = jnp.concatenate([quads[0][k], quads[1][k]], axis=0)
            pieces += [(both * keep + part_ref[k]).astype(jnp.bfloat16), whole_ref[k]]
        block = jnp.concatenate(pieces, axis=0)
        for one, part in enumerate(turn_pair(const_ref, block, (coarse, 8, 128))):
            both = jnp.concatenate([part, part], axis=1).astype(jnp.bfloat16)
            for p in range(2):
                pair = (2 * eight + one) * 2 + p
                placed = (both * masks[p]).reshape(2, coarse // 2, 16, 128)
                at = (slice(None), 1 - pair // 16, slice(None), pair % 16)
                out_ref[at] = late_ref[at] + placed


VMEM = pl.BlockSpec(memory_space=pltpu.VMEM)


def channelise_late(voltages, const):
    _, in_dev, coarse, samples = voltages.shape
    rows = in_dev * coarse
    return pl.pallas_call(
        late_kernel,
        in_specs=[VMEM, VMEM],
        out_specs=[VMEM, VMEM],
        out_shape=[
            jax.ShapeDtypeStruct((2, 2, coarse // 2, 16, 16, 128), jnp.bfloat16),
            jax.ShapeDtypeStruct((NFFT, 32, rows), jnp.float32),
        ],
        scratch_shapes=[pltpu.VMEM((NFFT, 128, rows), jnp.bfloat16)],
        compiler_params=pltpu.CompilerParams(vmem_limit_bytes=24 * MIB),
        cost_estimate=pl.CostEstimate(
            flops=2 * 256 * 2560 * 256 * 12, bytes_accessed=10 * MIB, transcendentals=0
        ),
        name="channelise_late",
    )(voltages, const)


def channelise_near(near, const, own):
    rows = own.shape[2]
    return pl.pallas_call(
        near_kernel,
        in_specs=[VMEM] * 3,
        out_specs=[VMEM] * 2,
        out_shape=[
            jax.ShapeDtypeStruct((NFFT, 16, rows), jnp.float32),
            jax.ShapeDtypeStruct((NFFT, 16, rows), jnp.bfloat16),
        ],
        compiler_params=pltpu.CompilerParams(vmem_limit_bytes=24 * MIB),
        cost_estimate=pl.CostEstimate(
            flops=2 * 256 * 2 * 256 * 7 * 256, bytes_accessed=4 * MIB, transcendentals=0
        ),
        name="channelise_near",
    )(near, const, own)


def channelise_far(far, const, late, part, whole):
    return pl.pallas_call(
        far_kernel,
        in_specs=[VMEM] * 5,
        out_specs=VMEM,
        out_shape=jax.ShapeDtypeStruct(late.shape, jnp.bfloat16),
        compiler_params=pltpu.CompilerParams(vmem_limit_bytes=24 * MIB),
        cost_estimate=pl.CostEstimate(
            flops=2 * 256 * 2 * 256 * 3 * 256, bytes_accessed=10 * MIB, transcendentals=0
        ),
        name="channelise_far",
    )(far, const, late, part, whole)


def correlate_kernel(scale, spec_ref, out_hbm, stage_ref, sems):
    sources, pairs = spec_ref.shape[:2]
    inputs = sources // 4 * 8
    lane = lax.broadcasted_iota(jnp.int32, (inputs, 128), 1)
    is_real = lane % (2 * QUAD) < QUAD

    def copy(channel):
        return pltpu.make_async_copy(stage_ref.at[channel], out_hbm.at[channel], sems.at[channel])

    def one_pair(pair, carry):
        block = spec_ref[:, pair].astype(jnp.float32).reshape(2, 2, sources // 8, 2, 2, 8, 128)
        for one in range(2):
            joined, turned = [], []
            for z_lo in range(2):
                for core in range(2):
                    upper, lower = block[:, z_lo, :, core, one].reshape(2, inputs // 2, 128)
                    plain = jnp.concatenate([lower, upper], axis=0)
                    ahead = pltpu.roll(plain, 128 - QUAD, 1)
                    behind = pltpu.roll(plain, QUAD, 1)
                    joined.append(plain.astype(jnp.bfloat16))
                    turned.append(jnp.where(is_real, ahead, -behind).astype(jnp.bfloat16))
            joined = jnp.concatenate(joined, axis=1)
            turned = jnp.concatenate(turned, axis=1)
            channel = 2 * pair + one
            for which, left in enumerate((joined, turned)):
                power = lax.dot_general(left, joined, NT, preferred_element_type=jnp.float32)
                stage_ref[channel, which] = power * scale
            copy(channel).start()
        return carry

    lax.fori_loop(0, pairs, one_pair, 0, unroll=4)
    for channel in range(2 * pairs):
        copy(channel).wait()


def correlate(spectra, scale):
    sources, pairs = spectra.shape[:2]
    inputs = sources // 4 * 8
    shape = (2 * pairs, 2, inputs, inputs)
    return pl.pallas_call(
        functools.partial(correlate_kernel, scale),
        in_specs=[pl.BlockSpec(memory_space=pltpu.VMEM)],
        out_specs=pl.BlockSpec(memory_space=pltpu.HBM),
        out_shape=jax.ShapeDtypeStruct(shape, jnp.float32),
        scratch_shapes=[
            pltpu.VMEM(shape, jnp.float32),
            pltpu.SemaphoreType.DMA((2 * pairs,)),
        ],
        compiler_params=pltpu.CompilerParams(vmem_limit_bytes=32 * MIB),
        cost_estimate=pl.CostEstimate(
            flops=2 * 16 * 2 * 256 * 256 * 512, bytes_accessed=12 * MIB, transcendentals=0
        ),
        name="correlate",
    )(spectra)


def body(voltages):
    samples = voltages.shape[3]
    scale = NFFT / (lax.axis_size(TIME) * samples)
    const = jnp.asarray(
        np.concatenate([make_weights(), make_swap(*voltages.shape[1:3])], axis=1)
    )
    middle = samples - HALO // 2
    near = from_behind(voltages[:, :, :, middle:], TIME, 1)
    far = from_behind(voltages[:, :, :, samples - HALO : middle], TIME, 1)
    late, own = channelise_late(voltages, const)
    spectra = channelise_far(far, const, late, *channelise_near(near, const, own))
    spectra = spectra.reshape(128, 8, 16, 128)
    moved = lax.all_to_all(
        spectra,
        STATION + TIME,
        split_axis=0,
        concat_axis=0,
        axis_index_groups=[PLANES_DOWN],
        tiled=True,
    )
    return correlate(moved, scale)


def solution(mesh):
    mesh = jax.sharding.Mesh(
        mesh.devices.reshape(2, 4, 4, 2, 2), ("z_hi", "y", "x", "z_lo", "core")
    )
    return jax.shard_map(
        body,
        mesh=mesh,
        in_specs=(P(None, STATION, None, TIME),),
        out_specs=P(STATION + TIME, None, None, None),
        check_vma=False,
    )
```

```python
import functools

import jax
import jax.numpy as jnp
import ml_dtypes
import numpy as np
from jax import lax
from jax.experimental import pallas as pl
from jax.experimental.pallas import tpu as pltpu
from jax.sharding import PartitionSpec as P

NFFT = 64
TAPS = 16
QUAD = 4
OCTET = 2 * QUAD * NFFT
WINDOW = (TAPS + QUAD) * NFFT
HALO = TAPS * NFFT
MIB = 1 << 20
NT = (((1,), (1,)), ((), ()))
VMEM = pl.BlockSpec(memory_space=pltpu.VMEM)
STATION = ("z_hi", "y", "x")
TIME = ("z_lo", "core")
PLANES_DOWN = [
    ((z_hi * 16 + chip) * 2 + z_lo) * 2 + core
    for z_hi in (1, 0)
    for z_lo in (1, 0)
    for chip in range(16)
    for core in range(2)
]


def from_behind(array, axis, by):
    size = lax.axis_size(axis)
    return lax.ppermute(array, axis, [(i, (i + by) % size) for i in range(size)])


def make_weights():
    length = TAPS * NFFT
    index = np.arange(length, dtype=np.float64)
    window = 0.5 - 0.5 * np.cos(2.0 * np.pi * (index + 0.5) / length)
    flat = np.sinc((index - (length - 1) / 2.0) / NFFT) * window
    taps = flat.reshape(TAPS, NFFT)
    gain = 1.0 / np.sqrt(np.sum(flat * flat))
    n = np.arange(NFFT)
    angle = -2.0 * np.pi * (n[:, None] * n[None, :] % NFFT) / NFFT
    cosine, sine = np.cos(angle) * gain, np.sin(angle) * gain
    table = np.stack([np.stack([cosine, sine], 1), np.stack([-sine, cosine], 1)], 0)
    table = table.astype(ml_dtypes.bfloat16).astype(np.float64)
    rows = table[:, :, :, : NFFT // 2].copy()
    rows[0, :, 1, 0] = table[0, :, 0, NFFT // 2]
    rows[1, :, 0, 0] = table[1, :, 1, NFFT // 2]
    weights = np.zeros((NFFT // 2, 2, QUAD, 2, TAPS + QUAD, NFFT))
    for spec in range(QUAD):
        for tap in range(TAPS):
            part = taps[tap][None, :, None, None] * rows
            weights[:, :, spec, :, spec + TAPS - tap, :] = part.transpose(3, 2, 0, 1)
    return weights.reshape(NFFT * QUAD, 2 * WINDOW).astype(ml_dtypes.bfloat16)


def make_swap(in_dev, coarse):
    size = in_dev * coarse
    swap = np.zeros((size, size))
    for i in range(in_dev):
        for c in range(coarse):
            swap[(c + coarse // 2) % coarse * in_dev + i, i * coarse + c] = 1.0
    return swap.astype(ml_dtypes.bfloat16)


def channels_from(weights, blocks):
    rows = blocks[0].shape[0]
    terms = [
        lax.dot_general(weight, block, NT, preferred_element_type=jnp.float32).reshape(
            NFFT // 2, 8, rows
        )
        for weight, block in zip(weights, blocks)
    ]
    upper = lax.broadcasted_iota(jnp.int32, (8, rows), 0) < QUAD
    channels = [None] * NFFT
    channels[0] = jnp.where(upper, terms[0][0], terms[1][0])
    channels[NFFT // 2] = pltpu.roll(jnp.where(upper, terms[1][0], terms[0][0]), QUAD, 0)
    for k in range(1, NFFT // 2):
        channels[k] = terms[0][k] + terms[1][k]
        difference = terms[0][k] - terms[1][k]
        channels[NFFT - k] = jnp.where(upper, difference, -difference)
    return channels


def quad_channels(samples, begin, width, const_ref, first):
    rows = samples[0].shape[0] * samples[0].shape[1]
    columns = [part * WINDOW + first for part in range(2)]
    return channels_from(
        [const_ref[:, column : column + width] for column in columns],
        [part[:, :, begin : begin + width].reshape(rows, width) for part in samples],
    )


def turn_pair(const_ref, block, out_shape):
    swap = const_ref[:, 2 * WINDOW : 2 * WINDOW + block.shape[1]]
    turned = lax.dot_general(swap, block, NT, preferred_element_type=jnp.float32)
    return [turned[:, one * 128 : (one + 1) * 128].reshape(out_shape) for one in range(2)]


def late_kernel(volt_ref, const_ref, out_ref, own_ref, spec_ref):
    octets = volt_ref.shape[3] // OCTET
    own = [volt_ref.at[part] for part in range(2)]
    rows = spec_ref.shape[2]
    step = QUAD * NFFT
    for k in range(NFFT):
        gap = 32 * (k % 4)
        spec_ref[k, gap : gap + 32] = jnp.zeros((32, rows), jnp.bfloat16)
    for octet in range(2, octets):
        quads = [
            quad_channels(own, (2 * octet + half) * step - HALO, WINDOW, const_ref, 0)
            for half in range(2)
        ]
        for k in range(NFFT):
            row = 16 * (octet - (0 if octet - 2 >= 2 * (k % 4) else 2))
            both = jnp.concatenate([quads[0][k], quads[1][k]], axis=0)
            spec_ref[k, row : row + 16] = both.astype(jnp.bfloat16)
    coarse = rows // 8

    for z_lo in range(2):

        def turn(pair, carry):
            block = spec_ref[pl.ds(32 * z_lo + 2 * pair, 2)].reshape(256, rows)
            both = turn_pair(const_ref, block, (coarse, 8, 128))
            both = jnp.concatenate(both, axis=1).astype(jnp.bfloat16)
            out_ref[:, 1 - z_lo, :, pair] = both.reshape(2, coarse // 2, 16, 128)
            return carry

        lax.fori_loop(0, NFFT // 4, turn, 0, unroll=8)
    for quad in range(4):
        width = (quad + 1) * step
        channels = quad_channels(own, 0, width, const_ref, WINDOW - width)
        for k in range(NFFT):
            own_ref[k, 8 * quad : 8 * quad + 8] = channels[k]


def keep_halo():
    return jnp.where(lax.axis_index(TIME) == 0, 0.0, 1.0)


def near_kernel(near_ref, const_ref, own_ref, part_ref, whole_ref):
    step = QUAD * NFFT
    near = [near_ref.at[part] for part in range(2)]
    keep = keep_halo()
    first = [
        quad_channels(near, 0, 2 * step, const_ref, (2 - quad) * step) for quad in range(2)
    ]
    second = [
        quad_channels(near, quad * step, (2 - quad) * step, const_ref, 0) for quad in range(2)
    ]
    for k in range(NFFT):
        both = jnp.concatenate([first[0][k], first[1][k]], axis=0)
        part_ref[k] = both * keep + own_ref[k, :16]
        both = jnp.concatenate([second[0][k], second[1][k]], axis=0)
        whole_ref[k] = (both * keep + own_ref[k, 16:]).astype(jnp.bfloat16)


def tail_kernel(volt_hbm, near_ref, far_ref, tail_ref, sems):
    samples = volt_hbm.shape[3]
    half = HALO // 2
    piece = lambda begin: volt_hbm.at[:, :, :, pl.ds(begin, half)]
    near = pltpu.make_async_copy(piece(samples - half), near_ref, sems.at[0])
    tail = pltpu.make_async_copy(piece(samples - HALO), tail_ref, sems.at[1])
    tail.start()
    near.start()
    tail.wait()
    in_dev, coarse = tail_ref.shape[1:3]
    real, imag = (
        tail_ref[part, :, :, :128].astype(jnp.float32).reshape(in_dev * coarse, 128)
        for part in range(2)
    )
    lane = lax.broadcasted_iota(jnp.int32, real.shape, 1)
    first = jnp.where(lane < NFFT, pltpu.roll(imag, NFFT, 1), real)
    far_ref[:, :, :128] = first.astype(jnp.bfloat16).reshape(in_dev, coarse, 128)
    far_ref[:, :, 128:half] = tail_ref[0, :, :, 128:]
    far_ref[:, :, half:] = tail_ref[1, :, :, 128:]
    near.wait()


def tails(voltages):
    _, in_dev, coarse, _ = voltages.shape
    half = HALO // 2
    return pl.pallas_call(
        tail_kernel,
        in_specs=[pl.BlockSpec(memory_space=pltpu.HBM)],
        out_specs=[VMEM] * 2,
        out_shape=[
            jax.ShapeDtypeStruct((2, in_dev, coarse, half), jnp.bfloat16),
            jax.ShapeDtypeStruct((in_dev, coarse, 2 * half - 128), jnp.bfloat16),
        ],
        scratch_shapes=[
            pltpu.VMEM((2, in_dev, coarse, half), jnp.bfloat16),
            pltpu.SemaphoreType.DMA((2,)),
        ],
        compiler_params=pltpu.CompilerParams(vmem_limit_bytes=50 * MIB),
        name="tails",
    )(voltages)


def far_kernel(far_ref, const_ref, late_ref, part_ref, whole_ref, out_ref):
    step = QUAD * NFFT
    half = 2 * step
    keep = keep_halo()
    packed = far_ref[...].reshape(part_ref.shape[2], 2 * half - 128)
    imag = jnp.concatenate([packed[:, :128], packed[:, half:]], axis=1)
    weight = jnp.concatenate(
        [const_ref[:, const_ref.shape[1] - 128 :], const_ref[:, WINDOW + 128 : WINDOW + half]],
        axis=1,
    )
    quads = [
        channels_from([const_ref[:, :half], weight], [packed[:, :half], imag]),
        channels_from(
            [const_ref[:, :step], const_ref[:, WINDOW : WINDOW + step]],
            [packed[:, step:half], imag[:, step:]],
        ),
    ]
    rows = part_ref.shape[2]
    coarse = rows // 8
    lane = lax.broadcasted_iota(jnp.int32, (16, 128), 1)
    second = lax.broadcasted_iota(jnp.int32, (16, 128), 0) // 8
    masks = [
        jnp.where(lane // 32 == 2 * p + second, 1.0, 0.0).astype(jnp.bfloat16) for p in range(2)
    ]
    for eight in range(NFFT // 8):
        pieces = []
        for k in range(8 * eight, 8 * eight + 8):
            both = jnp.concatenate([quads[0][k], quads[1][k]], axis=0)
            pieces += [(both * keep + part_ref[k]).astype(jnp.bfloat16), whole_ref[k]]
        block = jnp.concatenate(pieces, axis=0)
        for one, part in enumerate(turn_pair(const_ref, block, (coarse, 8, 128))):
            both = jnp.concatenate([part, part], axis=1).astype(jnp.bfloat16)
            for p in range(2):
                pair = (2 * eight + one) * 2 + p
                placed = (both * masks[p]).reshape(2, coarse // 2, 16, 128)
                at = (slice(None), 1 - pair // 16, slice(None), pair % 16)
                out_ref[at] = late_ref[at] + placed


def channelise_late(voltages, const):
    _, in_dev, coarse, samples = voltages.shape
    rows = in_dev * coarse
    return pl.pallas_call(
        late_kernel,
        in_specs=[VMEM, VMEM],
        out_specs=[VMEM, VMEM],
        out_shape=[
            jax.ShapeDtypeStruct((2, 2, coarse // 2, 16, 16, 128), jnp.bfloat16),
            jax.ShapeDtypeStruct((NFFT, 32, rows), jnp.float32),
        ],
        scratch_shapes=[pltpu.VMEM((NFFT, 128, rows), jnp.bfloat16)],
        compiler_params=pltpu.CompilerParams(vmem_limit_bytes=24 * MIB),
        cost_estimate=pl.CostEstimate(
            flops=2 * 256 * 2560 * 256 * 12, bytes_accessed=10 * MIB, transcendentals=0
        ),
        name="channelise_late",
    )(voltages, const)


def channelise_near(near, const, own):
    rows = own.shape[2]
    return pl.pallas_call(
        near_kernel,
        in_specs=[VMEM] * 3,
        out_specs=[VMEM] * 2,
        out_shape=[
            jax.ShapeDtypeStruct((NFFT, 16, rows), jnp.float32),
            jax.ShapeDtypeStruct((NFFT, 16, rows), jnp.bfloat16),
        ],
        compiler_params=pltpu.CompilerParams(vmem_limit_bytes=24 * MIB),
        cost_estimate=pl.CostEstimate(
            flops=2 * 256 * 2 * 256 * 7 * 256, bytes_accessed=4 * MIB, transcendentals=0
        ),
        name="channelise_near",
    )(near, const, own)


def channelise_far(far, const, late, part, whole):
    return pl.pallas_call(
        far_kernel,
        in_specs=[VMEM] * 5,
        out_specs=VMEM,
        out_shape=jax.ShapeDtypeStruct(late.shape, jnp.bfloat16),
        compiler_params=pltpu.CompilerParams(vmem_limit_bytes=24 * MIB),
        cost_estimate=pl.CostEstimate(
            flops=2 * 256 * 2 * 256 * 3 * 256, bytes_accessed=10 * MIB, transcendentals=0
        ),
        name="channelise_far",
    )(far, const, late, part, whole)


def correlate_kernel(scale, spec_ref, out_hbm, stage_ref, sems):
    sources, pairs = spec_ref.shape[:2]
    inputs = sources // 4 * 8
    lane = lax.broadcasted_iota(jnp.int32, (inputs, 128), 1)
    is_real = lane % (2 * QUAD) < QUAD

    def copy(channel):
        return pltpu.make_async_copy(stage_ref.at[channel], out_hbm.at[channel], sems.at[channel])

    def one_pair(pair, carry):
        block = spec_ref[:, pair].astype(jnp.float32).reshape(2, 2, sources // 8, 2, 2, 8, 128)
        for one in range(2):
            joined, turned = [], []
            for z_lo in range(2):
                for core in range(2):
                    upper, lower = block[:, z_lo, :, core, one].reshape(2, inputs // 2, 128)
                    plain = jnp.concatenate([lower, upper], axis=0)
                    ahead = pltpu.roll(plain, 128 - QUAD, 1)
                    behind = pltpu.roll(plain, QUAD, 1)
                    joined.append(plain.astype(jnp.bfloat16))
                    turned.append(jnp.where(is_real, ahead, -behind).astype(jnp.bfloat16))
            joined = jnp.concatenate(joined, axis=1)
            turned = jnp.concatenate(turned, axis=1)
            channel = 2 * pair + one
            for which, left in enumerate((joined, turned)):
                power = lax.dot_general(left, joined, NT, preferred_element_type=jnp.float32)
                stage_ref[channel, which] = power * scale
            copy(channel).start()
        return carry

    lax.fori_loop(0, pairs, one_pair, 0, unroll=4)
    for channel in range(2 * pairs):
        copy(channel).wait()


def correlate(spectra, scale):
    sources, pairs = spectra.shape[:2]
    inputs = sources // 4 * 8
    shape = (2 * pairs, 2, inputs, inputs)
    return pl.pallas_call(
        functools.partial(correlate_kernel, scale),
        in_specs=[pl.BlockSpec(memory_space=pltpu.VMEM)],
        out_specs=pl.BlockSpec(memory_space=pltpu.HBM),
        out_shape=jax.ShapeDtypeStruct(shape, jnp.float32),
        scratch_shapes=[
            pltpu.VMEM(shape, jnp.float32),
            pltpu.SemaphoreType.DMA((2 * pairs,)),
        ],
        compiler_params=pltpu.CompilerParams(vmem_limit_bytes=32 * MIB),
        cost_estimate=pl.CostEstimate(
            flops=2 * 16 * 2 * 256 * 256 * 512, bytes_accessed=12 * MIB, transcendentals=0
        ),
        name="correlate",
    )(spectra)


def body(voltages):
    samples = voltages.shape[3]
    scale = NFFT / (lax.axis_size(TIME) * samples)
    weights = make_weights()
    first = np.zeros_like(weights[:, :128])
    first[:, :NFFT] = weights[:, WINDOW + NFFT : WINDOW + 2 * NFFT]
    const = jnp.asarray(
        np.concatenate([weights, make_swap(*voltages.shape[1:3]), first], axis=1)
    )
    near, far = (from_behind(tail, TIME, 1) for tail in tails(voltages))
    late, own = channelise_late(voltages, const)
    spectra = channelise_far(far, const, late, *channelise_near(near, const, own))
    spectra = spectra.reshape(128, 8, 16, 128)
    moved = lax.all_to_all(
        spectra,
        STATION + TIME,
        split_axis=0,
        concat_axis=0,
        axis_index_groups=[PLANES_DOWN],
        tiled=True,
    )
    return correlate(moved, scale)


def solution(mesh):
    mesh = jax.sharding.Mesh(
        mesh.devices.reshape(2, 4, 4, 2, 2), ("z_hi", "y", "x", "z_lo", "core")
    )
    return jax.shard_map(
        body,
        mesh=mesh,
        in_specs=(P(None, STATION, None, TIME),),
        out_specs=P(STATION + TIME, None, None, None),
        check_vma=False,
    )
```

```python
import functools

import jax
import jax.numpy as jnp
import ml_dtypes
import numpy as np
from jax import lax
from jax.experimental import pallas as pl
from jax.experimental.pallas import tpu as pltpu
from jax.sharding import PartitionSpec as P

NFFT = 64
TAPS = 16
QUAD = 4
OCTET = 2 * QUAD * NFFT
WINDOW = (TAPS + QUAD) * NFFT
HALO = TAPS * NFFT
MIB = 1 << 20
NT = (((1,), (1,)), ((), ()))
VMEM = pl.BlockSpec(memory_space=pltpu.VMEM)
STATION = ("z_hi", "y", "x")
TIME = ("z_lo", "core")
PLANES_DOWN = [
    ((z_hi * 16 + chip) * 2 + z_lo) * 2 + core
    for z_hi in (1, 0)
    for z_lo in (1, 0)
    for chip in range(16)
    for core in range(2)
]


def from_behind(array, axis, by):
    size = lax.axis_size(axis)
    return lax.ppermute(array, axis, [(i, (i + by) % size) for i in range(size)])


def make_weights():
    length = TAPS * NFFT
    index = np.arange(length, dtype=np.float64)
    window = 0.5 - 0.5 * np.cos(2.0 * np.pi * (index + 0.5) / length)
    flat = np.sinc((index - (length - 1) / 2.0) / NFFT) * window
    taps = flat.reshape(TAPS, NFFT)
    gain = 1.0 / np.sqrt(np.sum(flat * flat))
    n = np.arange(NFFT)
    angle = -2.0 * np.pi * (n[:, None] * n[None, :] % NFFT) / NFFT
    cosine, sine = np.cos(angle) * gain, np.sin(angle) * gain
    table = np.stack([np.stack([cosine, sine], 1), np.stack([-sine, cosine], 1)], 0)
    table = table.astype(ml_dtypes.bfloat16).astype(np.float64)
    rows = table[:, :, :, : NFFT // 2].copy()
    rows[0, :, 1, 0] = table[0, :, 0, NFFT // 2]
    rows[1, :, 0, 0] = table[1, :, 1, NFFT // 2]
    weights = np.zeros((NFFT // 2, 2, QUAD, 2, TAPS + QUAD, NFFT))
    for spec in range(QUAD):
        for tap in range(TAPS):
            part = taps[tap][None, :, None, None] * rows
            weights[:, :, spec, :, spec + TAPS - tap, :] = part.transpose(3, 2, 0, 1)
    return weights.reshape(NFFT * QUAD, 2 * WINDOW).astype(ml_dtypes.bfloat16)


def make_swap(in_dev, coarse):
    size = in_dev * coarse
    swap = np.zeros((size, size))
    for i in range(in_dev):
        for c in range(coarse):
            swap[(c + coarse // 2) % coarse * in_dev + i, i * coarse + c] = 1.0
    return swap.astype(ml_dtypes.bfloat16)


def channels_from(weights, blocks):
    rows = blocks[0].shape[0]
    terms = [
        lax.dot_general(weight, block, NT, preferred_element_type=jnp.float32).reshape(
            NFFT // 2, 8, rows
        )
        for weight, block in zip(weights, blocks)
    ]
    upper = lax.broadcasted_iota(jnp.int32, (8, rows), 0) < QUAD
    channels = [None] * NFFT
    channels[0] = jnp.where(upper, terms[0][0], terms[1][0])
    channels[NFFT // 2] = pltpu.roll(jnp.where(upper, terms[1][0], terms[0][0]), QUAD, 0)
    for k in range(1, NFFT // 2):
        channels[k] = terms[0][k] + terms[1][k]
        difference = terms[0][k] - terms[1][k]
        channels[NFFT - k] = jnp.where(upper, difference, -difference)
    return channels


def quad_channels(samples, begin, width, const_ref, first):
    rows = samples[0].shape[0] * samples[0].shape[1]
    columns = [part * WINDOW + first for part in range(2)]
    return channels_from(
        [const_ref[:, column : column + width] for column in columns],
        [part[:, :, begin : begin + width].reshape(rows, width) for part in samples],
    )


def turn_pair(const_ref, block, out_shape):
    swap = const_ref[:, 2 * WINDOW : 2 * WINDOW + block.shape[1]]
    turned = lax.dot_general(swap, block, NT, preferred_element_type=jnp.float32)
    return [turned[:, one * 128 : (one + 1) * 128].reshape(out_shape) for one in range(2)]


def late_kernel(volt_ref, const_ref, out_ref, own_ref, spec_ref):
    octets = volt_ref.shape[3] // OCTET
    own = [volt_ref.at[part] for part in range(2)]
    rows = spec_ref.shape[2]
    step = QUAD * NFFT
    for k in range(NFFT):
        gap = 32 * (k // 2 % 4)
        spec_ref[k, gap : gap + 32] = jnp.zeros((32, rows), jnp.bfloat16)
    for octet in range(2, octets):
        quads = [
            quad_channels(own, (2 * octet + half) * step - HALO, WINDOW, const_ref, 0)
            for half in range(2)
        ]
        for k in range(NFFT):
            row = 16 * (octet - (0 if octet - 2 >= 2 * (k // 2 % 4) else 2))
            both = jnp.concatenate([quads[0][k], quads[1][k]], axis=0)
            spec_ref[k, row : row + 16] = both.astype(jnp.bfloat16)
    coarse = rows // 8

    for z_lo in range(2):

        def turn(pair, carry):
            block = spec_ref[pl.ds(32 * z_lo + 2 * pair, 2)].reshape(256, rows)
            both = turn_pair(const_ref, block, (coarse, 8, 128))
            both = jnp.concatenate(both, axis=1).astype(jnp.bfloat16)
            out_ref[:, 1 - z_lo, :, pair] = both.reshape(2, coarse // 2, 16, 128)
            return carry

        lax.fori_loop(0, NFFT // 4, turn, 0, unroll=8)
    for quad in range(4):
        width = (quad + 1) * step
        channels = quad_channels(own, 0, width, const_ref, WINDOW - width)
        for k in range(NFFT):
            own_ref[k, 8 * quad : 8 * quad + 8] = channels[k]


def keep_halo():
    return jnp.where(lax.axis_index(TIME) == 0, 0.0, 1.0)


def near_kernel(near_ref, const_ref, own_ref, part_ref, whole_ref):
    step = QUAD * NFFT
    near = [near_ref.at[part] for part in range(2)]
    keep = keep_halo()
    first = [
        quad_channels(near, 0, 2 * step, const_ref, (2 - quad) * step) for quad in range(2)
    ]
    second = [
        quad_channels(near, quad * step, (2 - quad) * step, const_ref, 0) for quad in range(2)
    ]
    for k in range(NFFT):
        both = jnp.concatenate([first[0][k], first[1][k]], axis=0)
        part_ref[k] = both * keep + own_ref[k, :16]
        both = jnp.concatenate([second[0][k], second[1][k]], axis=0)
        whole_ref[k] = (both * keep + own_ref[k, 16:]).astype(jnp.bfloat16)


def tail_kernel(volt_hbm, near_ref, far_ref, tail_ref, sems):
    samples = volt_hbm.shape[3]
    half = HALO // 2
    piece = lambda begin: volt_hbm.at[:, :, :, pl.ds(begin, half)]
    near = pltpu.make_async_copy(piece(samples - half), near_ref, sems.at[0])
    tail = pltpu.make_async_copy(piece(samples - HALO), tail_ref, sems.at[1])
    tail.start()
    near.start()
    tail.wait()
    in_dev, coarse = tail_ref.shape[1:3]
    real, imag = (
        tail_ref[part, :, :, :128].astype(jnp.float32).reshape(in_dev * coarse, 128)
        for part in range(2)
    )
    lane = lax.broadcasted_iota(jnp.int32, real.shape, 1)
    first = jnp.where(lane < NFFT, pltpu.roll(imag, NFFT, 1), real)
    far_ref[:, :, :128] = first.astype(jnp.bfloat16).reshape(in_dev, coarse, 128)
    far_ref[:, :, 128:half] = tail_ref[0, :, :, 128:]
    far_ref[:, :, half:] = tail_ref[1, :, :, 128:]
    near.wait()


def tails(voltages):
    _, in_dev, coarse, _ = voltages.shape
    half = HALO // 2
    return pl.pallas_call(
        tail_kernel,
        in_specs=[pl.BlockSpec(memory_space=pltpu.HBM)],
        out_specs=[VMEM] * 2,
        out_shape=[
            jax.ShapeDtypeStruct((2, in_dev, coarse, half), jnp.bfloat16),
            jax.ShapeDtypeStruct((in_dev, coarse, 2 * half - 128), jnp.bfloat16),
        ],
        scratch_shapes=[
            pltpu.VMEM((2, in_dev, coarse, half), jnp.bfloat16),
            pltpu.SemaphoreType.DMA((2,)),
        ],
        compiler_params=pltpu.CompilerParams(vmem_limit_bytes=50 * MIB),
        name="tails",
    )(voltages)


def far_kernel(far_ref, const_ref, late_ref, part_ref, whole_ref, out_ref):
    step = QUAD * NFFT
    half = 2 * step
    keep = keep_halo()
    packed = far_ref[...].reshape(part_ref.shape[2], 2 * half - 128)
    imag = jnp.concatenate([packed[:, :128], packed[:, half:]], axis=1)
    weight = jnp.concatenate(
        [const_ref[:, const_ref.shape[1] - 128 :], const_ref[:, WINDOW + 128 : WINDOW + half]],
        axis=1,
    )
    quads = [
        channels_from([const_ref[:, :half], weight], [packed[:, :half], imag]),
        channels_from(
            [const_ref[:, :step], const_ref[:, WINDOW : WINDOW + step]],
            [packed[:, step:half], imag[:, step:]],
        ),
    ]
    rows = part_ref.shape[2]
    coarse = rows // 8
    for eight in range(NFFT // 8):
        pieces = [[], []]
        for k in range(8 * eight, 8 * eight + 8):
            both = jnp.concatenate([quads[0][k], quads[1][k]], axis=0)
            both = (both * keep + part_ref[k]).astype(jnp.bfloat16)
            pieces[k % 2] += [both, whole_ref[k]]
        block = jnp.concatenate(pieces[0] + pieces[1], axis=0)
        both = jnp.concatenate(turn_pair(const_ref, block, (coarse, 8, 128)), axis=1)
        both = both.astype(jnp.bfloat16).reshape(2, coarse // 2, 16, 128)
        for one in range(4):
            pair = 4 * eight + one
            lanes = slice(32 * one, 32 * one + 32)
            out_ref[:, 1 - pair // 16, :, pair % 16, :, lanes] = both[:, :, :, lanes]


def channelise_late(voltages, const):
    _, in_dev, coarse, samples = voltages.shape
    rows = in_dev * coarse
    return pl.pallas_call(
        late_kernel,
        in_specs=[VMEM, VMEM],
        out_specs=[VMEM, VMEM],
        out_shape=[
            jax.ShapeDtypeStruct((2, 2, coarse // 2, 16, 16, 128), jnp.bfloat16),
            jax.ShapeDtypeStruct((NFFT, 32, rows), jnp.float32),
        ],
        scratch_shapes=[pltpu.VMEM((NFFT, 128, rows), jnp.bfloat16)],
        compiler_params=pltpu.CompilerParams(vmem_limit_bytes=24 * MIB),
        cost_estimate=pl.CostEstimate(
            flops=2 * 256 * 2560 * 256 * 12, bytes_accessed=10 * MIB, transcendentals=0
        ),
        name="channelise_late",
    )(voltages, const)


def channelise_near(near, const, own):
    rows = own.shape[2]
    return pl.pallas_call(
        near_kernel,
        in_specs=[VMEM] * 3,
        out_specs=[VMEM] * 2,
        out_shape=[
            jax.ShapeDtypeStruct((NFFT, 16, rows), jnp.float32),
            jax.ShapeDtypeStruct((NFFT, 16, rows), jnp.bfloat16),
        ],
        compiler_params=pltpu.CompilerParams(vmem_limit_bytes=24 * MIB),
        cost_estimate=pl.CostEstimate(
            flops=2 * 256 * 2 * 256 * 7 * 256, bytes_accessed=4 * MIB, transcendentals=0
        ),
        name="channelise_near",
    )(near, const, own)


def channelise_far(far, const, late, part, whole):
    return pl.pallas_call(
        far_kernel,
        in_specs=[VMEM] * 5,
        out_specs=VMEM,
        input_output_aliases={2: 0},
        out_shape=jax.ShapeDtypeStruct(late.shape, jnp.bfloat16),
        compiler_params=pltpu.CompilerParams(vmem_limit_bytes=24 * MIB),
        cost_estimate=pl.CostEstimate(
            flops=2 * 256 * 2 * 256 * 3 * 256, bytes_accessed=10 * MIB, transcendentals=0
        ),
        name="channelise_far",
    )(far, const, late, part, whole)


def correlate_kernel(scale, spec_ref, out_hbm, stage_ref, sems):
    sources, pairs = spec_ref.shape[:2]
    inputs = sources // 4 * 8
    lane = lax.broadcasted_iota(jnp.int32, (inputs, 128), 1)
    is_real = lane % (2 * QUAD) < QUAD

    def copy(channel):
        return pltpu.make_async_copy(stage_ref.at[channel], out_hbm.at[channel], sems.at[channel])

    def one_pair(pair, carry):
        block = spec_ref[:, pair].astype(jnp.float32).reshape(2, 2, sources // 8, 2, 2, 8, 128)
        for one in range(2):
            joined, turned = [], []
            for z_lo in range(2):
                for core in range(2):
                    upper, lower = block[:, z_lo, :, core, one].reshape(2, inputs // 2, 128)
                    plain = jnp.concatenate([lower, upper], axis=0)
                    ahead = pltpu.roll(plain, 128 - QUAD, 1)
                    behind = pltpu.roll(plain, QUAD, 1)
                    joined.append(plain.astype(jnp.bfloat16))
                    turned.append(jnp.where(is_real, ahead, -behind).astype(jnp.bfloat16))
            joined = jnp.concatenate(joined, axis=1)
            turned = jnp.concatenate(turned, axis=1)
            channel = 2 * pair + one
            for which, left in enumerate((joined, turned)):
                power = lax.dot_general(left, joined, NT, preferred_element_type=jnp.float32)
                stage_ref[channel, which] = power * scale
            copy(channel).start()
        return carry

    lax.fori_loop(0, pairs, one_pair, 0, unroll=4)
    for channel in range(2 * pairs):
        copy(channel).wait()


def correlate(spectra, scale):
    sources, pairs = spectra.shape[:2]
    inputs = sources // 4 * 8
    shape = (2 * pairs, 2, inputs, inputs)
    return pl.pallas_call(
        functools.partial(correlate_kernel, scale),
        in_specs=[pl.BlockSpec(memory_space=pltpu.VMEM)],
        out_specs=pl.BlockSpec(memory_space=pltpu.HBM),
        out_shape=jax.ShapeDtypeStruct(shape, jnp.float32),
        scratch_shapes=[
            pltpu.VMEM(shape, jnp.float32),
            pltpu.SemaphoreType.DMA((2 * pairs,)),
        ],
        compiler_params=pltpu.CompilerParams(vmem_limit_bytes=32 * MIB),
        cost_estimate=pl.CostEstimate(
            flops=2 * 16 * 2 * 256 * 256 * 512, bytes_accessed=12 * MIB, transcendentals=0
        ),
        name="correlate",
    )(spectra)


def body(voltages):
    samples = voltages.shape[3]
    scale = NFFT / (lax.axis_size(TIME) * samples)
    weights = make_weights()
    first = np.zeros_like(weights[:, :128])
    first[:, :NFFT] = weights[:, WINDOW + NFFT : WINDOW + 2 * NFFT]
    const = jnp.asarray(
        np.concatenate([weights, make_swap(*voltages.shape[1:3]), first], axis=1)
    )
    near, far = (from_behind(tail, TIME, 1) for tail in tails(voltages))
    late, own = channelise_late(voltages, const)
    spectra = channelise_far(far, const, late, *channelise_near(near, const, own))
    spectra = spectra.reshape(128, 8, 16, 128)
    moved = lax.all_to_all(
        spectra,
        STATION + TIME,
        split_axis=0,
        concat_axis=0,
        axis_index_groups=[PLANES_DOWN],
        tiled=True,
    )
    return correlate(moved, scale)


def solution(mesh):
    mesh = jax.sharding.Mesh(
        mesh.devices.reshape(2, 4, 4, 2, 2), ("z_hi", "y", "x", "z_lo", "core")
    )
    return jax.shard_map(
        body,
        mesh=mesh,
        in_specs=(P(None, STATION, None, TIME),),
        out_specs=P(STATION + TIME, None, None, None),
        check_vma=False,
    )
```

```python
import functools

import jax
import jax.numpy as jnp
import ml_dtypes
import numpy as np
from jax import lax
from jax.experimental import pallas as pl
from jax.experimental.pallas import tpu as pltpu
from jax.sharding import PartitionSpec as P

NFFT = 64
TAPS = 16
QUAD = 4
OCTET = 2 * QUAD * NFFT
WINDOW = (TAPS + QUAD) * NFFT
HALO = TAPS * NFFT
FAR = QUAD * NFFT
MIB = 1 << 20
NT = (((1,), (1,)), ((), ()))
VMEM = pl.BlockSpec(memory_space=pltpu.VMEM)
STATION = ("z_hi", "y", "x")
TIME = ("z_lo", "core")
PLANES_DOWN = [
    ((z_hi * 16 + chip) * 2 + z_lo) * 2 + core
    for z_hi in (1, 0)
    for z_lo in (1, 0)
    for chip in range(16)
    for core in range(2)
]


def from_behind(array, axis, by):
    size = lax.axis_size(axis)
    return lax.ppermute(array, axis, [(i, (i + by) % size) for i in range(size)])


def make_weights():
    length = TAPS * NFFT
    index = np.arange(length, dtype=np.float64)
    window = 0.5 - 0.5 * np.cos(2.0 * np.pi * (index + 0.5) / length)
    flat = np.sinc((index - (length - 1) / 2.0) / NFFT) * window
    taps = flat.reshape(TAPS, NFFT)
    gain = 1.0 / np.sqrt(np.sum(flat * flat))
    n = np.arange(NFFT)
    angle = -2.0 * np.pi * (n[:, None] * n[None, :] % NFFT) / NFFT
    cosine, sine = np.cos(angle) * gain, np.sin(angle) * gain
    table = np.stack([np.stack([cosine, sine], 1), np.stack([-sine, cosine], 1)], 0)
    table = table.astype(ml_dtypes.bfloat16).astype(np.float64)
    rows = table[:, :, :, : NFFT // 2].copy()
    rows[0, :, 1, 0] = table[0, :, 0, NFFT // 2]
    rows[1, :, 0, 0] = table[1, :, 1, NFFT // 2]
    weights = np.zeros((NFFT // 2, 2, QUAD, 2, TAPS + QUAD, NFFT))
    for spec in range(QUAD):
        for tap in range(TAPS):
            part = taps[tap][None, :, None, None] * rows
            weights[:, :, spec, :, spec + TAPS - tap, :] = part.transpose(3, 2, 0, 1)
    return weights.reshape(NFFT * QUAD, 2 * WINDOW).astype(ml_dtypes.bfloat16)


def make_swap(in_dev, coarse):
    size = in_dev * coarse
    swap = np.zeros((size, size))
    for i in range(in_dev):
        for c in range(coarse):
            swap[(c + coarse // 2) % coarse * in_dev + i, i * coarse + c] = 1.0
    return swap.astype(ml_dtypes.bfloat16)


def channels_from(weights, blocks):
    rows = blocks[0].shape[0]
    terms = [
        lax.dot_general(weight, block, NT, preferred_element_type=jnp.float32).reshape(
            NFFT // 2, 8, rows
        )
        for weight, block in zip(weights, blocks)
    ]
    upper = lax.broadcasted_iota(jnp.int32, (8, rows), 0) < QUAD
    channels = [None] * NFFT
    channels[0] = jnp.where(upper, terms[0][0], terms[1][0])
    channels[NFFT // 2] = pltpu.roll(jnp.where(upper, terms[1][0], terms[0][0]), QUAD, 0)
    for k in range(1, NFFT // 2):
        channels[k] = terms[0][k] + terms[1][k]
        difference = terms[0][k] - terms[1][k]
        channels[NFFT - k] = jnp.where(upper, difference, -difference)
    return channels


def quad_channels(samples, begin, width, const_ref, first):
    rows = samples[0].shape[0] * samples[0].shape[1]
    columns = [part * WINDOW + first for part in range(2)]
    return channels_from(
        [const_ref[:, column : column + width] for column in columns],
        [part[:, :, begin : begin + width].reshape(rows, width) for part in samples],
    )


def turn_pair(const_ref, block, out_shape):
    swap = const_ref[:, 2 * WINDOW : 2 * WINDOW + block.shape[1]]
    turned = lax.dot_general(swap, block, NT, preferred_element_type=jnp.float32)
    return [turned[:, one * 128 : (one + 1) * 128].reshape(out_shape) for one in range(2)]


def late_kernel(volt_ref, const_ref, out_ref, own_ref, spec_ref):
    octets = volt_ref.shape[3] // OCTET
    own = [volt_ref.at[part] for part in range(2)]
    rows = spec_ref.shape[2]
    step = QUAD * NFFT
    for k in range(NFFT):
        gap = 32 * (k // 2 % 4)
        spec_ref[k, gap : gap + 32] = jnp.zeros((32, rows), jnp.bfloat16)
    for octet in range(2, octets):
        quads = [
            quad_channels(own, (2 * octet + half) * step - HALO, WINDOW, const_ref, 0)
            for half in range(2)
        ]
        for k in range(NFFT):
            row = 16 * (octet - (0 if octet - 2 >= 2 * (k // 2 % 4) else 2))
            both = jnp.concatenate([quads[0][k], quads[1][k]], axis=0)
            spec_ref[k, row : row + 16] = both.astype(jnp.bfloat16)
    coarse = rows // 8

    for z_lo in range(2):

        def turn(pair, carry):
            block = spec_ref[pl.ds(32 * z_lo + 2 * pair, 2)].reshape(256, rows)
            both = turn_pair(const_ref, block, (coarse, 8, 128))
            both = jnp.concatenate(both, axis=1).astype(jnp.bfloat16)
            out_ref[:, 1 - z_lo, :, pair] = both.reshape(2, coarse // 2, 16, 128)
            return carry

        lax.fori_loop(0, NFFT // 4, turn, 0, unroll=8)
    for quad in range(4):
        width = (quad + 1) * step
        channels = quad_channels(own, 0, width, const_ref, WINDOW - width)
        for k in range(NFFT):
            own_ref[k, 8 * quad : 8 * quad + 8] = channels[k]


def keep_halo():
    return jnp.where(lax.axis_index(TIME) == 0, 0.0, 1.0)


def near_kernel(near_ref, const_ref, own_ref, part_ref, whole_ref):
    width = HALO - FAR
    near = [near_ref.at[part] for part in range(2)]
    keep = keep_halo()
    quads = [quad_channels(near, 0, width, const_ref, FAR)] + [
        quad_channels(near, quad * FAR, width - quad * FAR, const_ref, 0) for quad in range(3)
    ]
    for k in range(NFFT):
        both = jnp.concatenate([quads[0][k], quads[1][k]], axis=0)
        part_ref[k] = both * keep + own_ref[k, :16]
        both = jnp.concatenate([quads[2][k], quads[3][k]], axis=0)
        whole_ref[k] = (both * keep + own_ref[k, 16:]).astype(jnp.bfloat16)


def tail_kernel(volt_hbm, near_ref, far_ref, tail_ref, sems):
    begin = volt_hbm.shape[3] - HALO
    piece = lambda first, size: volt_hbm.at[:, :, :, pl.ds(first, size)]
    near = pltpu.make_async_copy(piece(begin + FAR, HALO - FAR), near_ref, sems.at[0])
    tail = pltpu.make_async_copy(piece(begin, FAR), tail_ref, sems.at[1])
    tail.start()
    near.start()
    tail.wait()
    in_dev, coarse = tail_ref.shape[1:3]
    real, imag = (
        tail_ref[part, :, :, :128].astype(jnp.float32).reshape(in_dev * coarse, 128)
        for part in range(2)
    )
    lane = lax.broadcasted_iota(jnp.int32, real.shape, 1)
    first = jnp.where(lane < NFFT, pltpu.roll(imag, NFFT, 1), real)
    far_ref[:, :, :128] = first.astype(jnp.bfloat16).reshape(in_dev, coarse, 128)
    far_ref[:, :, 128:FAR] = tail_ref[0, :, :, 128:]
    far_ref[:, :, FAR:] = tail_ref[1, :, :, 128:]
    near.wait()


def tails(voltages):
    _, in_dev, coarse, _ = voltages.shape
    return pl.pallas_call(
        tail_kernel,
        in_specs=[pl.BlockSpec(memory_space=pltpu.HBM)],
        out_specs=[VMEM] * 2,
        out_shape=[
            jax.ShapeDtypeStruct((2, in_dev, coarse, HALO - FAR), jnp.bfloat16),
            jax.ShapeDtypeStruct((in_dev, coarse, 2 * FAR - 128), jnp.bfloat16),
        ],
        scratch_shapes=[
            pltpu.VMEM((2, in_dev, coarse, FAR), jnp.bfloat16),
            pltpu.SemaphoreType.DMA((2,)),
        ],
        compiler_params=pltpu.CompilerParams(vmem_limit_bytes=50 * MIB),
        name="tails",
    )(voltages)


def far_kernel(far_ref, const_ref, late_ref, part_ref, whole_ref, out_ref):
    keep = keep_halo()
    packed = far_ref[...].reshape(part_ref.shape[2], 2 * FAR - 128)
    imag = jnp.concatenate([packed[:, :128], packed[:, FAR:]], axis=1)
    weight = jnp.concatenate(
        [const_ref[:, const_ref.shape[1] - 128 :], const_ref[:, WINDOW + 128 : WINDOW + FAR]],
        axis=1,
    )
    quad = channels_from([const_ref[:, :FAR], weight], [packed[:, :FAR], imag])
    rows = part_ref.shape[2]
    coarse = rows // 8
    for eight in range(NFFT // 8):
        pieces = [[], []]
        for k in range(8 * eight, 8 * eight + 8):
            both = jnp.concatenate([quad[k] * keep + part_ref[k, :8], part_ref[k, 8:]], axis=0)
            both = both.astype(jnp.bfloat16)
            pieces[k % 2] += [both, whole_ref[k]]
        block = jnp.concatenate(pieces[0] + pieces[1], axis=0)
        both = jnp.concatenate(turn_pair(const_ref, block, (coarse, 8, 128)), axis=1)
        both = both.astype(jnp.bfloat16).reshape(2, coarse // 2, 16, 128)
        for one in range(4):
            pair = 4 * eight + one
            lanes = slice(32 * one, 32 * one + 32)
            out_ref[:, 1 - pair // 16, :, pair % 16, :, lanes] = both[:, :, :, lanes]


def channelise_late(voltages, const):
    _, in_dev, coarse, samples = voltages.shape
    rows = in_dev * coarse
    return pl.pallas_call(
        late_kernel,
        in_specs=[VMEM, VMEM],
        out_specs=[VMEM, VMEM],
        out_shape=[
            jax.ShapeDtypeStruct((2, 2, coarse // 2, 16, 16, 128), jnp.bfloat16),
            jax.ShapeDtypeStruct((NFFT, 32, rows), jnp.float32),
        ],
        scratch_shapes=[pltpu.VMEM((NFFT, 128, rows), jnp.bfloat16)],
        compiler_params=pltpu.CompilerParams(vmem_limit_bytes=24 * MIB),
        cost_estimate=pl.CostEstimate(
            flops=2 * 256 * 2560 * 256 * 12, bytes_accessed=10 * MIB, transcendentals=0
        ),
        name="channelise_late",
    )(voltages, const)


def channelise_near(near, const, own):
    rows = own.shape[2]
    return pl.pallas_call(
        near_kernel,
        in_specs=[VMEM] * 3,
        out_specs=[VMEM] * 2,
        out_shape=[
            jax.ShapeDtypeStruct((NFFT, 16, rows), jnp.float32),
            jax.ShapeDtypeStruct((NFFT, 16, rows), jnp.bfloat16),
        ],
        compiler_params=pltpu.CompilerParams(vmem_limit_bytes=24 * MIB),
        cost_estimate=pl.CostEstimate(
            flops=2 * 256 * 2 * 256 * 7 * 256, bytes_accessed=4 * MIB, transcendentals=0
        ),
        name="channelise_near",
    )(near, const, own)


def channelise_far(far, const, late, part, whole):
    return pl.pallas_call(
        far_kernel,
        in_specs=[VMEM] * 5,
        out_specs=VMEM,
        input_output_aliases={2: 0},
        out_shape=jax.ShapeDtypeStruct(late.shape, jnp.bfloat16),
        compiler_params=pltpu.CompilerParams(vmem_limit_bytes=24 * MIB),
        cost_estimate=pl.CostEstimate(
            flops=2 * 256 * 2 * 256 * 3 * 256, bytes_accessed=10 * MIB, transcendentals=0
        ),
        name="channelise_far",
    )(far, const, late, part, whole)


def correlate_kernel(scale, spec_ref, out_hbm, stage_ref, sems):
    sources, pairs = spec_ref.shape[:2]
    inputs = sources // 4 * 8
    lane = lax.broadcasted_iota(jnp.int32, (inputs, 128), 1)
    is_real = lane % (2 * QUAD) < QUAD

    def copy(channel):
        return pltpu.make_async_copy(stage_ref.at[channel], out_hbm.at[channel], sems.at[channel])

    def one_pair(pair, carry):
        block = spec_ref[:, pair].astype(jnp.float32).reshape(2, 2, sources // 8, 2, 2, 8, 128)
        for one in range(2):
            joined, turned = [], []
            for z_lo in range(2):
                for core in range(2):
                    upper, lower = block[:, z_lo, :, core, one].reshape(2, inputs // 2, 128)
                    plain = jnp.concatenate([lower, upper], axis=0)
                    ahead = pltpu.roll(plain, 128 - QUAD, 1)
                    behind = pltpu.roll(plain, QUAD, 1)
                    joined.append(plain.astype(jnp.bfloat16))
                    turned.append(jnp.where(is_real, ahead, -behind).astype(jnp.bfloat16))
            joined = jnp.concatenate(joined, axis=1)
            turned = jnp.concatenate(turned, axis=1)
            channel = 2 * pair + one
            for which, left in enumerate((joined, turned)):
                power = lax.dot_general(left, joined, NT, preferred_element_type=jnp.float32)
                stage_ref[channel, which] = power * scale
            copy(channel).start()
        return carry

    lax.fori_loop(0, pairs, one_pair, 0, unroll=4)
    for channel in range(2 * pairs):
        copy(channel).wait()


def correlate(spectra, scale):
    sources, pairs = spectra.shape[:2]
    inputs = sources // 4 * 8
    shape = (2 * pairs, 2, inputs, inputs)
    return pl.pallas_call(
        functools.partial(correlate_kernel, scale),
        in_specs=[pl.BlockSpec(memory_space=pltpu.VMEM)],
        out_specs=pl.BlockSpec(memory_space=pltpu.HBM),
        out_shape=jax.ShapeDtypeStruct(shape, jnp.float32),
        scratch_shapes=[
            pltpu.VMEM(shape, jnp.float32),
            pltpu.SemaphoreType.DMA((2 * pairs,)),
        ],
        compiler_params=pltpu.CompilerParams(vmem_limit_bytes=32 * MIB),
        cost_estimate=pl.CostEstimate(
            flops=2 * 16 * 2 * 256 * 256 * 512, bytes_accessed=12 * MIB, transcendentals=0
        ),
        name="correlate",
    )(spectra)


def body(voltages):
    samples = voltages.shape[3]
    scale = NFFT / (lax.axis_size(TIME) * samples)
    weights = make_weights()
    first = np.zeros_like(weights[:, :128])
    first[:, :NFFT] = weights[:, WINDOW + NFFT : WINDOW + 2 * NFFT]
    const = jnp.asarray(
        np.concatenate([weights, make_swap(*voltages.shape[1:3]), first], axis=1)
    )
    near, far = (from_behind(tail, TIME, 1) for tail in tails(voltages))
    late, own = channelise_late(voltages, const)
    spectra = channelise_far(far, const, late, *channelise_near(near, const, own))
    spectra = spectra.reshape(128, 8, 16, 128)
    moved = lax.all_to_all(
        spectra,
        STATION + TIME,
        split_axis=0,
        concat_axis=0,
        axis_index_groups=[PLANES_DOWN],
        tiled=True,
    )
    return correlate(moved, scale)


def solution(mesh):
    mesh = jax.sharding.Mesh(
        mesh.devices.reshape(2, 4, 4, 2, 2), ("z_hi", "y", "x", "z_lo", "core")
    )
    return jax.shard_map(
        body,
        mesh=mesh,
        in_specs=(P(None, STATION, None, TIME),),
        out_specs=P(STATION + TIME, None, None, None),
        check_vma=False,
    )
```
